512 devices in a mesh: row: 2 (over core), circ: 32 (over z, x), ax: 8 (over y).
Axes of the slice: x: 4, y: 8, z: 8, core: 2. Of those that a mesh axis runs over, the one named last changes fastest.
Arguments:
- state: float32 [2, 5, 128, 1024, 128], P('row', None, 'ax', 'circ'), may hold values from -6 to 42, as said below
- rotor_step: int32 [1], replicated, may hold values from 0 to 99999
Outputs:
- advanced: float32 [2, 5, 128, 1024, 128], P('row', None, 'ax', 'circ')
- coupled_modes: float32 [2, 128, 5, 2, 128], P('row', 'circ', None, None, 'ax')
The draws below stay inside these ranges and needn't reach their ends.
Inputs may be any that keep to these rules, and one draw needn't show every extreme that they name: Density lies in 0.7 to 1.3 and the pressure the state implies in 0.5 to 1.7. `rotor_step`: circumferential pitches the rotor has turned.
All inputs are finite; a program needn't handle non-finite values.
Results may differ from the reference program's by a relative error of at most 0.000082.
Values sent between devices are 32-bit elements; how exact they have to be, the bound alone decides.
A program may use at most 192 MiB of HBM per device.

```python
import math
import jax
import jax.numpy as jnp
from jax import lax

CR = 128
MODES = 128
NA = 128
NT = 1024


def hot_envelope(key):
    spot_keys = jax.random.split(key, 3)
    centre_axial = jax.random.randint(spot_keys[0], (2, 1, 1, 1), 0, NA)
    centre_circ = jax.random.randint(spot_keys[1], (2, 1, 1, 1), 0, NT)
    height = 2.0 + jax.random.uniform(spot_keys[2], (2, 1, 1, 1), jnp.float32)
    axial_gap = (jnp.arange(NA, dtype=jnp.int32).reshape(1, NA, 1, 1) - centre_axial).astype(jnp.float32)
    circ_gap = jnp.abs(jnp.arange(NT, dtype=jnp.int32).reshape(1, 1, NT, 1) - centre_circ)
    circ_gap = jnp.minimum(circ_gap, NT - circ_gap).astype(jnp.float32)
    return 1.0 + height * jnp.exp(-(axial_gap * axial_gap + circ_gap * circ_gap) / 8.0)


def draw_state(key, part):
    key = jax.random.fold_in(key, 11)
    subkeys = jax.random.split(key, 6)
    full_shape = (2, NA, NT, CR)
    envelope = hot_envelope(subkeys[5])
    uniforms = [jax.random.uniform(subkeys[member], full_shape, jnp.float32) for member in range(5)]
    density = 0.8 + 0.4 * uniforms[0]
    vel_axial = envelope * (2.0 * uniforms[1] - 1.0)
    vel_circ = envelope * (2.0 * uniforms[2] - 1.0)
    vel_radial = envelope * (2.0 * uniforms[3] - 1.0)
    pressure = 0.6 + uniforms[4]
    energy = pressure / 0.4 + 0.5 * density * (vel_axial * vel_axial + vel_circ * vel_circ + vel_radial * vel_radial)
    return jnp.stack([density, density * vel_axial, density * vel_circ, density * vel_radial, energy], axis=1)


def setup_inputs(seed: int = 0) -> dict:
    streams_of = jax.random.split(jax.random.key(seed), 3)
    state = draw_state(jax.random.fold_in(streams_of[2], 71), 0)
    rotor_step = jax.random.randint(streams_of[1], (1,), 0, 100000).astype(jnp.int32)
    return dict(state=state, rotor_step=rotor_step)


courant = 0.8
two_pi = 2.0 * math.pi

def primitive(state):
    density = state[0]
    vel_axial = state[1] / density
    vel_circ = state[2] / density
    vel_radial = state[3] / density
    pressure = 0.4 * (state[4] - 0.5 * (state[1] * vel_axial + state[2] * vel_circ + state[3] * vel_radial))
    return (density, (vel_axial, vel_circ, vel_radial), pressure)

def fluxes(state, direction):
    density, velocity, pressure = primitive(state)
    moving = velocity[direction]
    components = [state[0] * moving, state[1] * moving, state[2] * moving, state[3] * moving, state[4] * moving + pressure * moving]
    components[1 + direction] = components[1 + direction] + pressure
    return jnp.stack(components)

def wave_speed(state):
    density, velocity, pressure = primitive(state)
    sound_speed = jnp.sqrt(1.4 * pressure / density)
    fastest = jnp.maximum(jnp.maximum(jnp.abs(velocity[0]), jnp.abs(velocity[1])), jnp.abs(velocity[2]))
    return jnp.max(fastest + sound_speed)

def advance(state, axial_ext, axial_flux, circ_ext, circ_flux, speed_max):
    radial_ext = jnp.concatenate([state[..., :1], state, state[..., -1:]], axis=3)
    radial_flux = fluxes(radial_ext, 2)
    convection = (axial_flux[:, 2:] - axial_flux[:, :-2]) * 0.5
    convection = convection + (circ_flux[:, :, 2:] - circ_flux[:, :, :-2]) * 0.5
    convection = convection + (radial_flux[..., 2:] - radial_flux[..., :-2]) * 0.5
    smoothing = axial_ext[:, 2:] - 2.0 * state + axial_ext[:, :-2]
    smoothing = smoothing + (circ_ext[:, :, 2:] - 2.0 * state + circ_ext[:, :, :-2])
    smoothing = smoothing + (radial_ext[..., 2:] - 2.0 * state + radial_ext[..., :-2])
    time_step = courant / (3.0 * speed_max)
    return state - time_step * convection + courant / 6.0 * smoothing

def basis(mode_first, mode_count, cell_first, cell_count, total_cells):
    mode_index = mode_first + lax.iota(jnp.int32, mode_count)
    cell_index = cell_first + lax.iota(jnp.int32, cell_count)
    phase_index = mode_index[:, None] * cell_index[None, :] % total_cells
    angles = phase_index.astype(jnp.float32) * (two_pi / total_cells)
    norm_scale = math.sqrt(2.0 / total_cells)
    return (jnp.cos(angles) * norm_scale, -jnp.sin(angles) * norm_scale)

def project(interface, cosines, sines):
    real_part = jnp.einsum('mj,fjr->mfr', cosines, interface, precision=lax.Precision.HIGHEST)
    imag_part = jnp.einsum('mj,fjr->mfr', sines, interface, precision=lax.Precision.HIGHEST)
    return jnp.stack([real_part, imag_part], axis=2)

def rotate(coeffs, mode_first, rotor_step, orient, total_cells):
    mode_index = mode_first + lax.iota(jnp.int32, coeffs.shape[0])
    phase_index = mode_index * rotor_step[0] % total_cells
    angles = phase_index.astype(jnp.float32) * (two_pi / total_cells)
    cosine = jnp.cos(angles)[:, None, None]
    sine_part = jnp.sin(angles)[:, None, None]
    real_part = coeffs[:, :, 0]
    imag_part = coeffs[:, :, 1]
    new_real = real_part * cosine - orient * imag_part * sine_part
    new_imag = orient * real_part * sine_part + imag_part * cosine
    return jnp.stack([new_real, new_imag], axis=2)

def reference(state, rotor_step):
    speed_max = jnp.max(lax.map(wave_speed, state))

    def one_row(row_state):
        axial_ext = jnp.concatenate([row_state[:, :1], row_state, row_state[:, -1:]], axis=1)
        circ_ext = jnp.concatenate([row_state[:, :, -1:], row_state, row_state[:, :, :1]], axis=2)
        return advance(row_state, axial_ext, fluxes(axial_ext, 0), circ_ext, fluxes(circ_ext, 1), speed_max)
    advanced = lax.map(one_row, state)
    planes = advanced[:, :, NA - 1]
    cosines, sines = basis(0, MODES, 0, NT, NT)
    from_rotor = rotate(project(planes[0], cosines, sines), 0, rotor_step, 1.0, NT)
    from_stator = rotate(project(planes[1], cosines, sines), 0, rotor_step, -1.0, NT)
    coupled_modes = jnp.stack([from_stator, from_rotor])
    return (advanced, coupled_modes)
```

```python
import functools
import math

import jax
import jax.numpy as jnp
import numpy as np
from jax import lax
from jax.experimental import pallas as pl
from jax.experimental.pallas import tpu as pltpu
from jax.sharding import PartitionSpec as P

MESH = pl.DeviceIdType.MESH
F32 = jnp.float32
FIELDS = 5
MODES_HERE = 4
ROWS = 40
DEPTH = 128
SMOOTH = 0.8 / 6.0


def tables(circ, cells):
    total = circ * cells
    sector = np.arange(circ)[:, None]
    position = np.zeros((circ, ROWS), np.int64)
    position[:, :cells] = sector * cells + np.arange(cells)[None]
    position[:, cells] = sector[:, 0] * cells + cells
    position[:, cells + 1] = sector[:, 0] * cells - 1
    valid = np.arange(ROWS) < cells + 2
    owner, part, inner = np.meshgrid(np.arange(circ), np.arange(2), np.arange(MODES_HERE), indexing="ij")
    mode = (owner * MODES_HERE + inner).reshape(-1)
    part = part.reshape(-1)
    phase = (mode[None, :, None] * position[:, None, :]) % total
    angle = phase * (2.0 * math.pi / total)
    value = np.where(part[None, :, None] == 0, np.cos(angle), -np.sin(angle)) * math.sqrt(2.0 / total)
    value = np.where(valid[None, None], value, 0.0).astype(np.float32)
    high = value.astype(jnp.bfloat16).astype(np.float32)
    low = (value - high).astype(jnp.bfloat16).astype(np.float32)
    rest = np.zeros((circ, value.shape[1], DEPTH - 3 * ROWS), np.float32)
    return np.concatenate([high, high, low, rest], axis=2)


def flux(q, w, d, f):
    value = q[f] * w[d]
    if f == 1 + d:
        value = value + w[3]
    if f == 4:
        value = value + w[3] * w[d]
    return value


def primitive(q):
    inverse = 1.0 / q[0]
    u = [q[1 + d] * inverse for d in range(3)]
    p = 0.4 * (q[4] - 0.5 * (q[1] * u[0] + q[2] * u[1] + q[3] * u[2]))
    return u + [p], inverse


def lanes_next(v, lane):
    return jnp.where(lane == 127, v, pltpu.roll(v, 127, 1))


def lanes_prev(v, lane):
    return jnp.where(lane == 0, v, pltpu.roll(v, 1, 1))


def comm_kernel(
    circ, ax,
    st, rot, tab, adv, modes,
    S, W, GA, GC, WG, CS, conv, E, MB, XR, PS, R, MA, RA, MM, RB,
    rotor, load_sem, tab_sem, rot_sem, ga_send, ga_recv, gc_send, gc_recv,
    x_send, x_recv, a_send, a_recv, b_send, b_recv, m_send, m_recv,
):
    r, c, y = lax.axis_index("row"), lax.axis_index("circ"), lax.axis_index("ax")
    na, nt = S.shape[1] - 2, S.shape[2]
    last = ax - 1
    load = pltpu.make_async_copy(st.at[0], S.at[:, pl.ds(1, na)], load_sem)
    load.start()
    table = pltpu.make_async_copy(tab.at[c], E, tab_sem)
    table.start()
    turn = pltpu.make_async_copy(rot, rotor, rot_sem)
    turn.start()

    def near(k):
        return (lax.rem(r + k // ax, 2), c, lax.rem(y + lax.rem(k, ax), ax))

    def far(k):
        return (1 - r, lax.rem(c + k, circ), y)

    right, left = (r, lax.rem(c + 1, circ), y), (r, lax.rem(c + circ - 1, circ), y)
    barrier = pltpu.get_barrier_semaphore()

    def greet(device):
        pl.semaphore_signal(barrier, inc=1, device_id=device, device_id_type=MESH)

    def loop(lo, hi, body):
        def step(i, carry):
            body(i)
            return carry

        lax.fori_loop(lo, hi, step, 0)

    loop(1, 2 * ax, lambda k: greet(near(k)))
    loop(1, circ, lambda k: greet(far(k)))
    greet(right)
    greet(left)

    load.wait()

    def speeds(a, fastest):
        q = [S[f, a] for f in range(FIELDS)]
        w, inverse = primitive(q)
        for i in range(4):
            W[i, a] = w[i]
        speed = jnp.maximum(jnp.maximum(jnp.abs(w[0]), jnp.abs(w[1])), jnp.abs(w[2]))
        speed = speed + jnp.sqrt(1.4 * w[3] * inverse)
        for i in range(nt // 8):
            fastest = jnp.maximum(fastest, speed[8 * i : 8 * i + 8])
        return fastest

    MA[...] = lax.fori_loop(1, na + 1, speeds, jnp.zeros((8, 128), F32))
    for f in range(FIELDS):
        CS[0, f] = S[f, 1 : na + 1, nt - 1]
        CS[1, f] = S[f, 1 : na + 1, 0]

    lane = lax.broadcasted_iota(jnp.int32, (nt, 128), 1)
    cell = lax.broadcasted_iota(jnp.int32, (nt, 128), 0)

    @pl.when(y == last)
    def _():
        q = [S[f, na] for f in range(FIELDS)]
        w = [W[i, na] for i in range(4)]
        qm = [S[f, na - 1] for f in range(FIELDS)]
        wm = [W[i, na - 1] for i in range(4)]
        edge = lax.broadcasted_iota(jnp.int32, (8, 128), 0)
        wide = lax.broadcasted_iota(jnp.int32, (ROWS, 128), 1)

        def inside_next(v):
            return jnp.where(cell == nt - 1, 0.0, pltpu.roll(v, nt - 1, 0))

        def inside_prev(v):
            return jnp.where(cell == 0, 0.0, pltpu.roll(v, 1, 0))

        for f in range(FIELDS):
            qf = q[f]
            smooth = qm[f] - 5.0 * qf + lanes_next(qf, lane) + lanes_prev(qf, lane)
            smooth = smooth + inside_next(qf) + inside_prev(qf)
            still = qf + SMOOTH * smooth
            f1, f2 = flux(q, w, 1, f), flux(q, w, 2, f)
            moved = flux(q, w, 0, f) - flux(qm, wm, 0, f)
            moved = moved + lanes_next(f2, lane) - lanes_prev(f2, lane)
            moved = 0.5 * (moved + inside_next(f1) - inside_prev(f1))
            q_ends = jnp.where(edge == 0, qf[nt - 1 : nt], jnp.where(edge == 1, qf[0:1], 0.0))
            f_ends = jnp.where(edge == 0, -f1[nt - 1 : nt], jnp.where(edge == 1, f1[0:1], 0.0))
            pair = [
                jnp.concatenate([still, SMOOTH * q_ends], axis=0),
                jnp.concatenate([moved, 0.5 * f_ends], axis=0),
            ]
            band = 128 // ax
            for part in range(2):

                def cut(k, carry, part=part, f=f):
                    shift = lax.rem(band * f + 128 - band * k, 128)
                    turned = pltpu.roll(pair[part], shift, 1)
                    if f == 0:
                        MB[k, part] = turned
                    else:
                        MB[k, part] = jnp.where(wide // band == f, turned, MB[k, part])
                    return carry

                lax.fori_loop(0, ax, cut, 0)
        XR[...] = MB[last]

    pl.semaphore_wait(barrier, 2 * ax - 1 + circ - 1 + 2)

    def send(src, dst, sent, got, device):
        return pltpu.make_async_remote_copy(
            src_ref=src, dst_ref=dst, send_sem=sent, recv_sem=got, device_id=device, device_id_type=MESH
        )

    def drain(ref, sem):
        pltpu.make_async_copy(ref, ref, sem).wait()

    loop(1, 2 * ax, lambda k: send(MA, RA.at[k], a_send, a_recv, near(k)).start())

    @pl.when(y == last)
    def _():
        loop(0, last, lambda k: send(MB.at[k], XR, x_send, x_recv, (r, c, k)).start())

    gc_right = send(CS.at[0], GC.at[0], gc_send.at[0], gc_recv.at[0], right)
    gc_left = send(CS.at[1], GC.at[1], gc_send.at[1], gc_recv.at[1], left)
    gc_right.start()
    gc_left.start()
    ga_up = send(S.at[:, na], GA.at[0], ga_send.at[0], ga_recv.at[0], (r, c, lax.rem(y + 1, ax)))
    ga_down = send(S.at[:, 1], GA.at[1], ga_send.at[1], ga_recv.at[1], (r, c, lax.rem(y + last, ax)))
    ga_up.start()
    ga_down.start()

    drain(RA.at[pl.ds(1, 2 * ax - 1)], a_recv)
    MM[...] = lax.fori_loop(1, 2 * ax, lambda k, m: jnp.maximum(m, RA[k]), MA[...])
    loop(1, circ, lambda k: send(MM, RB.at[k], b_send, b_recv, far(k)).start())

    table.wait()

    @pl.when(y != last)
    def _():
        drain(XR, x_recv)

    x = jnp.concatenate([XR[0], XR[1]], axis=1)
    high = x.astype(jnp.bfloat16).astype(F32)
    stack = jnp.concatenate([high, x - high, high, jnp.zeros((DEPTH - 3 * ROWS, 256), F32)], axis=0)
    PS[...] = jnp.dot(E[...].astype(jnp.bfloat16), stack.astype(jnp.bfloat16), preferred_element_type=F32)

    def share(k):
        owner = lax.rem(c + k, circ)
        rows = pl.ds(pl.multiple_of(owner * 8, 8), 8)
        send(PS.at[rows], R.at[k], m_send, m_recv, far(k)).start()

    loop(0, circ, share)

    gc_right.wait_recv()
    gc_left.wait_recv()
    for side in range(2):
        w, _ = primitive([GC[side, f] for f in range(FIELDS)])
        for i in range(4):
            WG[side, i] = w[i]
    ga_up.wait_recv()
    ga_down.wait_recv()
    low_end, high_end = y == 0, y == last
    for f in range(FIELDS):
        S[f, 0] = jnp.where(low_end, S[f, 1], GA[0, f])
        S[f, na + 1] = jnp.where(high_end, S[f, na], GA[1, f])
    for a in (0, na + 1):
        w, _ = primitive([S[f, a] for f in range(FIELDS)])
        for i in range(4):
            W[i, a] = w[i]

    def plane(a, carry):
        q = [S[f, a] for f in range(FIELDS)]
        w = [W[i, a] for i in range(4)]
        row = pl.ds(a - 1, 1)
        gq = [[GC[side, f, row] for f in range(FIELDS)] for side in range(2)]
        gw = [[WG[side, i, row] for i in range(4)] for side in range(2)]
        qu, wu = [S[f, a + 1] for f in range(FIELDS)], [W[i, a + 1] for i in range(4)]
        qd, wd = [S[f, a - 1] for f in range(FIELDS)], [W[i, a - 1] for i in range(4)]
        for f in range(FIELDS):

            def cells_next(v, g):
                return jnp.where(cell == nt - 1, g, pltpu.roll(v, nt - 1, 0))

            def cells_prev(v, g):
                return jnp.where(cell == 0, g, pltpu.roll(v, 1, 0))

            qf = q[f]
            smooth = qu[f] + qd[f] - 6.0 * qf + lanes_next(qf, lane) + lanes_prev(qf, lane)
            smooth = smooth + cells_next(qf, gq[1][f]) + cells_prev(qf, gq[0][f])
            adv[0, f, a - 1] = qf + SMOOTH * smooth
            f1, f2 = flux(q, w, 1, f), flux(q, w, 2, f)
            moved = flux(qu, wu, 0, f) - flux(qd, wd, 0, f)
            moved = moved + lanes_next(f2, lane) - lanes_prev(f2, lane)
            moved = moved + cells_next(f1, flux(gq[1], gw[1], 1, f)) - cells_prev(f1, flux(gq[0], gw[0], 1, f))
            conv[f, a - 1] = 0.5 * moved
        return carry

    lax.fori_loop(1, na + 1, plane, 0)

    turn.wait()
    mode = c * MODES_HERE + lax.rem(lax.broadcasted_iota(jnp.int32, (8, 128), 0), MODES_HERE)
    total = circ * nt
    angle = ((mode * rotor[0, 0]) & (total - 1)).astype(F32) * (2.0 * math.pi / total)
    imaginary = lax.broadcasted_iota(jnp.int32, (8, 128), 0) >= MODES_HERE
    orient = (2 * r - 1).astype(F32)
    cosine = jnp.cos(angle)
    sine = jnp.where(imaginary, orient, -orient) * jnp.sin(angle)

    drain(RB.at[pl.ds(1, circ - 1)], b_recv)
    fastest = lax.fori_loop(1, circ, lambda k, m: jnp.maximum(m, RB[k]), MM[...])
    step = 0.8 / (3.0 * jnp.full((8, 128), jnp.max(fastest), F32))
    step_plane = jnp.concatenate([step] * (nt // 8), axis=0)

    def finish(a):
        for f in range(FIELDS):
            adv[0, f, a] = adv[0, f, a] - step_plane * conv[f, a]

    loop(0, na, finish)

    drain(R, m_recv)
    sums = lax.fori_loop(0, circ, lambda k, s: s + R[k], jnp.zeros((8, 256), F32))
    own = sums[:, :128] - step * sums[:, 128:]
    modes[...] = own * cosine + pltpu.roll(own, MODES_HERE, 0) * sine

    drain(RA.at[pl.ds(1, 2 * ax - 1)], a_send)
    drain(RB.at[pl.ds(1, circ - 1)], b_send)
    drain(R, m_send)

    @pl.when(y == last)
    def _():
        drain(MB.at[pl.ds(0, last)], x_send)

    for copy in (gc_right, gc_left, ga_up, ga_down):
        copy.wait_send()


def finish_kernel(adv, turned, out, modes, sem):
    copy = pltpu.make_async_copy(adv, out, sem)
    copy.start()
    value = turned[...]
    band = modes.shape[-1]
    for f in range(FIELDS):
        here = pltpu.roll(value, 128 - band * f, 1) if f else value
        for i in range(MODES_HERE):
            for part in range(2):
                row = part * MODES_HERE + i
                modes[0, i, f, part : part + 1] = here[row : row + 1, :band]
    copy.wait()


def on_device(circ, ax, state, rotor_step):
    na, nt = state.shape[2], state.shape[3]
    table = jnp.asarray(tables(circ, nt))
    hbm = pl.BlockSpec(memory_space=pltpu.HBM)
    vmem = pl.BlockSpec(memory_space=pltpu.VMEM)
    dma = pltpu.SemaphoreType.DMA
    block = (FIELDS, na, nt, 128)
    adv, turned = pl.pallas_call(
        functools.partial(comm_kernel, circ, ax),
        out_shape=[pltpu.VMEM(state.shape, F32), pltpu.VMEM((8, 128), F32)],
        in_specs=[hbm, hbm, hbm],
        out_specs=[vmem, vmem],
        scratch_shapes=[
            pltpu.VMEM((FIELDS, na + 2, nt, 128), F32),
            pltpu.VMEM((4, na + 2, nt, 128), F32),
            pltpu.VMEM((2, FIELDS, nt, 128), F32),
            pltpu.VMEM((2, FIELDS, na, 128), F32),
            pltpu.VMEM((2, 4, na, 128), F32),
            pltpu.VMEM((2, FIELDS, na, 128), F32),
            pltpu.VMEM(block, F32),
            pltpu.VMEM((circ * 8, DEPTH), F32),
            pltpu.VMEM((ax, 2, ROWS, 128), F32),
            pltpu.VMEM((2, ROWS, 128), F32),
            pltpu.VMEM((circ * 8, 256), F32),
            pltpu.VMEM((circ, 8, 256), F32),
            pltpu.VMEM((8, 128), F32),
            pltpu.VMEM((2 * ax, 8, 128), F32),
            pltpu.VMEM((8, 128), F32),
            pltpu.VMEM((circ, 8, 128), F32),
            pltpu.SMEM((1, 1), jnp.int32),
            dma, dma, dma, dma((2,)), dma((2,)), dma((2,)), dma((2,)),
            dma, dma, dma, dma, dma, dma, dma, dma,
        ],
        compiler_params=pltpu.CompilerParams(
            collective_id=0, has_side_effects=True, vmem_limit_bytes=56 * 2**20
        ),
        name="exchange",
    )(state, rotor_step.reshape(1, 1), table)
    return pl.pallas_call(
        finish_kernel,
        out_shape=[
            jax.ShapeDtypeStruct(state.shape, F32),
            jax.ShapeDtypeStruct((1, MODES_HERE, FIELDS, 2, 128 // ax), F32),
        ],
        in_specs=[vmem, vmem],
        out_specs=[hbm, vmem],
        scratch_shapes=[dma],
        name="finish",
    )(adv, turned)


def solution(mesh):
    return jax.shard_map(
        functools.partial(on_device, mesh.shape["circ"], mesh.shape["ax"]),
        mesh=mesh,
        in_specs=(P("row", None, "ax", "circ", None), P()),
        out_specs=(P("row", None, "ax", "circ", None), P("row", "circ", None, None, "ax")),
        check_vma=False,
    )
```

```python
import functools
import math

import jax
import jax.numpy as jnp
import numpy as np
from jax import lax
from jax.experimental import pallas as pl
from jax.experimental.pallas import tpu as pltpu
from jax.sharding import PartitionSpec as P

MESH = pl.DeviceIdType.MESH
F32 = jnp.float32
FIELDS = 5
MODES_HERE = 4
ROWS = 40
DEPTH = 128
SMOOTH = 0.8 / 6.0
EARLY = 0


def tables(circ, cells):
    total = circ * cells
    sector = np.arange(circ)[:, None]
    position = np.zeros((circ, ROWS), np.int64)
    position[:, :cells] = sector * cells + np.arange(cells)[None]
    position[:, cells] = sector[:, 0] * cells + cells
    position[:, cells + 1] = sector[:, 0] * cells - 1
    valid = np.arange(ROWS) < cells + 2
    owner, part, inner = np.meshgrid(np.arange(circ), np.arange(2), np.arange(MODES_HERE), indexing="ij")
    mode = (owner * MODES_HERE + inner).reshape(-1)
    part = part.reshape(-1)
    phase = (mode[None, :, None] * position[:, None, :]) % total
    angle = phase * (2.0 * math.pi / total)
    value = np.where(part[None, :, None] == 0, np.cos(angle), -np.sin(angle)) * math.sqrt(2.0 / total)
    value = np.where(valid[None, None], value, 0.0).astype(np.float32)
    high = value.astype(jnp.bfloat16).astype(np.float32)
    low = (value - high).astype(jnp.bfloat16).astype(np.float32)
    rest = np.zeros((circ, value.shape[1], DEPTH - 3 * ROWS), np.float32)
    return np.concatenate([high, high, low, rest], axis=2)


def flux(q, w, d, f):
    value = q[f] * w[d]
    if f == 1 + d:
        value = value + w[3]
    if f == 4:
        value = value + w[3] * w[d]
    return value


def primitive(q):
    inverse = 1.0 / q[0]
    u = [q[1 + d] * inverse for d in range(3)]
    p = 0.4 * (q[4] - 0.5 * (q[1] * u[0] + q[2] * u[1] + q[3] * u[2]))
    return u + [p], inverse


def lanes_next(v, lane):
    return jnp.where(lane == 127, v, pltpu.roll(v, 127, 1))


def lanes_prev(v, lane):
    return jnp.where(lane == 0, v, pltpu.roll(v, 1, 1))


def distance(n, d):
    return min(d, n - d)


def offsets(first, second):
    pairs = [(d, e) for d in range(first) for e in range(second)]
    return sorted(pairs, key=lambda p: (-distance(first, p[0]) - distance(second, p[1]), p == (0, 0)))


def comm_kernel(
    circ, across, ax,
    st, rot, tab, adv, modes,
    S, W, GA, GC, KG, CS, conv, E, MB, XR, PS, R, MA, RA, MM, RB,
    rotor, load_sem, tab_sem, rot_sem, ga_send, ga_recv, gc_send, gc_recv,
    x_send, x_recv, a_send, a_recv, b_send, b_recv, m_send, m_recv,
):
    r, c, y = lax.axis_index("row"), lax.axis_index("circ"), lax.axis_index("ax")
    na, nt = S.shape[1] - 2, S.shape[2]
    last = ax - 1
    load = pltpu.make_async_copy(st.at[0], S.at[:, pl.ds(1, na)], load_sem)
    load.start()
    table = pltpu.make_async_copy(tab.at[c], E, tab_sem)
    table.start()
    turn = pltpu.make_async_copy(rot, rotor, rot_sem)
    turn.start()

    along = circ // across
    lines = [lax.rem(y + d, ax) for d in range(ax)]
    layers = [lax.rem(c // across + d, along) * across for d in range(along)]
    columns = [lax.rem(lax.rem(c, across) + d, across) for d in range(across)]
    near_offsets, far_offsets = offsets(ax, 2), offsets(along, across)

    def near(i):
        d, e = near_offsets[i]
        return (1 - r if e else r, c, lines[d])

    def sector(i):
        d, e = far_offsets[i]
        return layers[d] + columns[e]

    def far(i):
        return (1 - r, sector(i), y)

    right, left = (r, lax.rem(c + 1, circ), y), (r, lax.rem(c + circ - 1, circ), y)
    barrier = pltpu.get_barrier_semaphore()

    def greet(device):
        pl.semaphore_signal(barrier, inc=1, device_id=device, device_id_type=MESH)

    def loop(lo, hi, body):
        def step(i, carry):
            body(i)
            return carry

        lax.fori_loop(lo, hi, step, 0)

    for i in range(circ // 2):
        greet(far(i))
    for i in range(2 * ax - 1):
        greet(near(i))
    for i in range(circ // 2, circ - 1):
        greet(far(i))
    greet(right)
    greet(left)

    load.wait()

    def speeds(a, fastest):
        q = [S[f, a] for f in range(FIELDS)]
        w, inverse = primitive(q)
        for i in range(4):
            W[i, a] = w[i]
        speed = jnp.maximum(jnp.maximum(jnp.abs(w[0]), jnp.abs(w[1])), jnp.abs(w[2]))
        speed = speed + jnp.sqrt(1.4 * w[3] * inverse)
        for i in range(nt // 8):
            fastest = jnp.maximum(fastest, speed[8 * i : 8 * i + 8])
        return fastest

    MA[...] = lax.fori_loop(1, na + 1, speeds, jnp.zeros((8, 128), F32))
    for f in range(FIELDS):
        CS[0, f] = S[f, 1 : na + 1, nt - 1]
        CS[1, f] = S[f, 1 : na + 1, 0]

    lane = lax.broadcasted_iota(jnp.int32, (nt, 128), 1)
    cell = lax.broadcasted_iota(jnp.int32, (nt, 128), 0)
    edge = lax.broadcasted_iota(jnp.int32, (8, 128), 0)

    def inside_next(v):
        return jnp.where(cell == nt - 1, 0.0, pltpu.roll(v, nt - 1, 0))

    def inside_prev(v):
        return jnp.where(cell == 0, 0.0, pltpu.roll(v, 1, 0))

    def plane(a):
        q, w = [S[f, a] for f in range(FIELDS)], [W[i, a] for i in range(4)]
        qu, wu = [S[f, a + 1] for f in range(FIELDS)], [W[i, a + 1] for i in range(4)]
        qd, wd = [S[f, a - 1] for f in range(FIELDS)], [W[i, a - 1] for i in range(4)]
        for f in range(FIELDS):
            qf = q[f]
            smooth = qu[f] + qd[f] - 6.0 * qf + lanes_next(qf, lane) + lanes_prev(qf, lane)
            adv[0, f, a - 1] = qf + SMOOTH * (smooth + inside_next(qf) + inside_prev(qf))
            f1, f2 = flux(q, w, 1, f), flux(q, w, 2, f)
            moved = flux(qu, wu, 0, f) - flux(qd, wd, 0, f)
            moved = moved + lanes_next(f2, lane) - lanes_prev(f2, lane)
            conv[f, a - 1] = 0.5 * (moved + inside_next(f1) - inside_prev(f1))

    for a in (0, na + 1):
        for f in range(FIELDS):
            S[f, a] = jnp.zeros((nt, 128), F32)
        for i in range(4):
            W[i, a] = jnp.zeros((nt, 128), F32)

    band = 128 // ax

    @pl.when(y == last)
    def _():
        q = [S[f, na] for f in range(FIELDS)]
        w = [W[i, na] for i in range(4)]
        qm = [S[f, na - 1] for f in range(FIELDS)]
        wm = [W[i, na - 1] for i in range(4)]
        group = lax.broadcasted_iota(jnp.int32, (ROWS, 128), 1) // band
        terms = [[], []]
        for f in range(FIELDS):
            qf = q[f]
            smooth = qm[f] - 5.0 * qf + lanes_next(qf, lane) + lanes_prev(qf, lane)
            smooth = smooth + inside_next(qf) + inside_prev(qf)
            still = qf + SMOOTH * smooth
            f1, f2 = flux(q, w, 1, f), flux(q, w, 2, f)
            moved = flux(q, w, 0, f) - flux(qm, wm, 0, f)
            moved = moved + lanes_next(f2, lane) - lanes_prev(f2, lane)
            moved = 0.5 * (moved + inside_next(f1) - inside_prev(f1))
            q_ends = jnp.where(edge == 0, qf[nt - 1 : nt], jnp.where(edge == 1, qf[0:1], 0.0))
            f_ends = jnp.where(edge == 0, -f1[nt - 1 : nt], jnp.where(edge == 1, f1[0:1], 0.0))
            for part, (inner, ends) in enumerate(((still, SMOOTH * q_ends), (moved, 0.5 * f_ends))):
                whole = jnp.concatenate([inner, ends], axis=0)
                terms[part].append(pltpu.roll(whole, band * f, 1) if f else whole)
        for k in range(ax):
            for part in range(2):
                chosen = terms[part][0]
                for f in range(1, FIELDS):
                    chosen = jnp.where(group == (f + k) % ax, terms[part][f], chosen)
                MB[k, part] = pltpu.roll(chosen, 128 - band * k, 1) if k else chosen
        XR[...] = MB[last]

    loop(1, 1 + EARLY, plane)
    pl.semaphore_wait(barrier, 2 * ax - 1 + circ - 1 + 2)

    def send(src, dst, sent, got, device):
        return pltpu.make_async_remote_copy(
            src_ref=src, dst_ref=dst, send_sem=sent, recv_sem=got, device_id=device, device_id_type=MESH
        )

    def drain(ref, sem):
        pltpu.make_async_copy(ref, ref, sem).wait()

    for i in range(2 * ax - 1):
        send(MA, RA.at[i], a_send, a_recv, near(i)).start()

    @pl.when(y == last)
    def _():
        for k in sorted(range(last), key=lambda k: -distance(ax, last - k)):
            send(MB.at[k], XR, x_send, x_recv, (r, c, k)).start()

    gc_right = send(CS.at[0], GC.at[0], gc_send.at[0], gc_recv.at[0], right)
    gc_left = send(CS.at[1], GC.at[1], gc_send.at[1], gc_recv.at[1], left)
    gc_right.start()
    gc_left.start()
    ga_up = send(S.at[:, na], GA.at[0], ga_send.at[0], ga_recv.at[0], (r, c, lax.rem(y + 1, ax)))
    ga_down = send(S.at[:, 1], GA.at[1], ga_send.at[1], ga_recv.at[1], (r, c, lax.rem(y + last, ax)))
    ga_up.start()
    ga_down.start()

    loop(1 + EARLY, na + 1, plane)
    drain(RA.at[pl.ds(0, 2 * ax - 1)], a_recv)
    MM[...] = lax.fori_loop(0, 2 * ax - 1, lambda i, m: jnp.maximum(m, RA[i]), MA[...])
    for i in range(circ - 1):
        send(MM, RB.at[i], b_send, b_recv, far(i)).start()

    table.wait()

    @pl.when(y != last)
    def _():
        drain(XR, x_recv)

    x = jnp.concatenate([XR[0], XR[1]], axis=1)
    high = x.astype(jnp.bfloat16).astype(F32)
    stack = jnp.concatenate([high, x - high, high, jnp.zeros((DEPTH - 3 * ROWS, 256), F32)], axis=0)
    PS[...] = jnp.dot(E[...].astype(jnp.bfloat16), stack.astype(jnp.bfloat16), preferred_element_type=F32)

    for i in range(circ):
        rows = pl.ds(pl.multiple_of(sector(i) * 8, 8), 8)
        send(PS.at[rows], R.at[i], m_send, m_recv, far(i)).start()

    turn.wait()
    mode = c * MODES_HERE + lax.rem(lax.broadcasted_iota(jnp.int32, (8, 128), 0), MODES_HERE)
    total = circ * nt
    angle = ((mode * rotor[0, 0]) & (total - 1)).astype(F32) * (2.0 * math.pi / total)
    imaginary = lax.broadcasted_iota(jnp.int32, (8, 128), 0) >= MODES_HERE
    orient = (2 * r - 1).astype(F32)
    cosine = jnp.cos(angle)
    sine = jnp.where(imaginary, orient, -orient) * jnp.sin(angle)

    ga_up.wait_recv()
    ga_down.wait_recv()
    for side, a, sign, alone in ((0, 0, -0.5, y == 0), (1, na - 1, 0.5, y == last)):
        ghost = [jnp.where(alone, S[f, a + 1], GA[side, f]) for f in range(FIELDS)]
        w, _ = primitive(ghost)
        for f in range(FIELDS):
            adv[0, f, a] = adv[0, f, a] + SMOOTH * ghost[f]
            conv[f, a] = conv[f, a] + sign * flux(ghost, w, 0, f)
    gc_right.wait_recv()
    gc_left.wait_recv()

    drain(RB.at[pl.ds(0, circ - 1)], b_recv)
    fastest = lax.fori_loop(0, circ - 1, lambda i, m: jnp.maximum(m, RB[i]), MM[...])
    step = 0.8 / (3.0 * jnp.full((8, 128), jnp.max(fastest), F32))
    step_plane = jnp.concatenate([step] * (nt // 8), axis=0)

    for side, sign in ((0, 0.5), (1, -0.5)):
        ghost = [GC[side, f] for f in range(FIELDS)]
        w, _ = primitive(ghost)
        weight = jnp.concatenate([sign * step] * (na // 8), axis=0)
        for f in range(FIELDS):
            KG[side, f] = SMOOTH * ghost[f] + weight * flux(ghost, w, 1, f)

    def finish(a):
        row = pl.ds(a, 1)
        for f in range(FIELDS):
            value = adv[0, f, a] - step_plane * conv[f, a]
            first = jnp.where(edge == 0, KG[0, f, row], 0.0)
            final = jnp.where(edge == 7, KG[1, f, row], 0.0)
            adv[0, f, a, 0:8] = value[0:8] + first
            adv[0, f, a, 8 : nt - 8] = value[8 : nt - 8]
            adv[0, f, a, nt - 8 : nt] = value[nt - 8 : nt] + final

    loop(0, na, finish)

    drain(R, m_recv)
    sums = lax.fori_loop(0, circ, lambda k, s: s + R[k], jnp.zeros((8, 256), F32))
    own = sums[:, :128] - step * sums[:, 128:]
    modes[...] = own * cosine + pltpu.roll(own, MODES_HERE, 0) * sine

    drain(RA.at[pl.ds(0, 2 * ax - 1)], a_send)
    drain(RB.at[pl.ds(0, circ - 1)], b_send)
    drain(R, m_send)

    @pl.when(y == last)
    def _():
        drain(MB.at[pl.ds(0, last)], x_send)

    for copy in (gc_right, gc_left, ga_up, ga_down):
        copy.wait_send()


def finish_kernel(adv, turned, out, out_modes, modes, sems):
    copies = [pltpu.make_async_copy(adv.at[0, f], out.at[0, f], sems.at[f]) for f in range(FIELDS)]
    for copy in copies:
        copy.start()
    value = turned[...]
    band = modes.shape[-1]
    for f in range(FIELDS):
        here = pltpu.roll(value, 128 - band * f, 1) if f else value
        for i in range(MODES_HERE):
            for part in range(2):
                row = part * MODES_HERE + i
                modes[0, i, f, part : part + 1] = here[row : row + 1, :band]
    copies.append(pltpu.make_async_copy(modes, out_modes, sems.at[FIELDS]))
    copies[-1].start()
    for copy in copies:
        copy.wait()


def on_device(circ, ax, state, rotor_step):
    na, nt = state.shape[2], state.shape[3]
    table = jnp.asarray(tables(circ, nt))
    hbm = pl.BlockSpec(memory_space=pltpu.HBM)
    vmem = pl.BlockSpec(memory_space=pltpu.VMEM)
    dma = pltpu.SemaphoreType.DMA
    block = (FIELDS, na, nt, 128)
    adv, turned = pl.pallas_call(
        functools.partial(comm_kernel, circ, 4 if circ % 4 == 0 else 1, ax),
        out_shape=[pltpu.VMEM(state.shape, F32), pltpu.VMEM((8, 128), F32)],
        in_specs=[hbm, hbm, hbm],
        out_specs=[vmem, vmem],
        scratch_shapes=[
            pltpu.VMEM((FIELDS, na + 2, nt, 128), F32),
            pltpu.VMEM((4, na + 2, nt, 128), F32),
            pltpu.VMEM((2, FIELDS, nt, 128), F32),
            pltpu.VMEM((2, FIELDS, na, 128), F32),
            pltpu.VMEM((2, FIELDS, na, 128), F32),
            pltpu.VMEM((2, FIELDS, na, 128), F32),
            pltpu.VMEM(block, F32),
            pltpu.VMEM((circ * 8, DEPTH), F32),
            pltpu.VMEM((ax, 2, ROWS, 128), F32),
            pltpu.VMEM((2, ROWS, 128), F32),
            pltpu.VMEM((circ * 8, 256), F32),
            pltpu.VMEM((circ, 8, 256), F32),
            pltpu.VMEM((8, 128), F32),
            pltpu.VMEM((2 * ax, 8, 128), F32),
            pltpu.VMEM((8, 128), F32),
            pltpu.VMEM((circ, 8, 128), F32),
            pltpu.SMEM((1, 1), jnp.int32),
            dma, dma, dma, dma((2,)), dma((2,)), dma((2,)), dma((2,)),
            dma, dma, dma, dma, dma, dma, dma, dma,
        ],
        compiler_params=pltpu.CompilerParams(
            collective_id=0, has_side_effects=True, vmem_limit_bytes=56 * 2**20
        ),
        name="exchange",
    )(state, rotor_step.reshape(1, 1), table)
    return pl.pallas_call(
        finish_kernel,
        out_shape=[
            jax.ShapeDtypeStruct(state.shape, F32),
            jax.ShapeDtypeStruct((1, MODES_HERE, FIELDS, 2, 128 // ax), F32),
        ],
        in_specs=[vmem, vmem],
        out_specs=[hbm, hbm],
        scratch_shapes=[pltpu.VMEM((1, MODES_HERE, FIELDS, 2, 128 // ax), F32), dma((FIELDS + 1,))],
        compiler_params=pltpu.CompilerParams(vmem_limit_bytes=16 * 2**20),
        name="finish",
    )(pltpu.with_memory_space_constraint(adv, pltpu.VMEM), pltpu.with_memory_space_constraint(turned, pltpu.VMEM))


def solution(mesh):
    return jax.shard_map(
        functools.partial(on_device, mesh.shape["circ"], mesh.shape["ax"]),
        mesh=mesh,
        in_specs=(P("row", None, "ax", "circ", None), P()),
        out_specs=(P("row", None, "ax", "circ", None), P("row", "circ", None, None, "ax")),
        check_vma=False,
    )
```

```python
import functools
import math

import jax
import jax.numpy as jnp
import numpy as np
from jax import lax
from jax.experimental import pallas as pl
from jax.experimental.pallas import tpu as pltpu
from jax.sharding import PartitionSpec as P

MESH = pl.DeviceIdType.MESH
F32 = jnp.float32
FIELDS = 5
MODES_HERE = 4
ROWS = 40
DEPTH = 128
BAND_ROWS = 48
SENT = 11
SMOOTH = 0.8 / 6.0
EARLY = 0


def tables(circ, cells):
    total = circ * cells
    sector = np.arange(circ)[:, None]
    position = np.zeros((circ, ROWS), np.int64)
    position[:, :cells] = sector * cells + np.arange(cells)[None]
    position[:, cells] = sector[:, 0] * cells + cells
    position[:, cells + 1] = sector[:, 0] * cells - 1
    valid = np.arange(ROWS) < cells + 2
    owner, inner, part = np.meshgrid(np.arange(circ), np.arange(MODES_HERE), np.arange(2), indexing="ij")
    mode = (owner * MODES_HERE + inner).reshape(-1)
    part = part.reshape(-1)
    phase = (mode[None, :, None] * position[:, None, :]) % total
    angle = phase * (2.0 * math.pi / total)
    value = np.where(part[None, :, None] == 0, np.cos(angle), -np.sin(angle)) * math.sqrt(2.0 / total)
    value = np.where(valid[None, None], value, 0.0).astype(np.float32)
    high = value.astype(jnp.bfloat16).astype(np.float32)
    low = (value - high).astype(jnp.bfloat16).astype(np.float32)
    rest = np.zeros((circ, value.shape[1], DEPTH - 3 * ROWS), np.float32)
    return np.concatenate([high, high, low, rest], axis=2)


def flux(q, w, d, f):
    value = q[f] * w[d]
    if f == 1 + d:
        value = value + w[3]
    if f == 4:
        value = value + w[3] * w[d]
    return value


def primitive(q):
    inverse = 1.0 / q[0]
    u = [q[1 + d] * inverse for d in range(3)]
    p = 0.4 * (q[4] - 0.5 * (q[1] * u[0] + q[2] * u[1] + q[3] * u[2]))
    return u + [p], inverse


def lanes_next(v, lane):
    return jnp.where(lane == 127, v, pltpu.roll(v, 127, 1))


def lanes_prev(v, lane):
    return jnp.where(lane == 0, v, pltpu.roll(v, 1, 1))


def distance(n, d):
    return min(d, n - d)


def offsets(first, second):
    pairs = [(d, e) for d in range(first) for e in range(second)]
    return sorted(pairs, key=lambda p: (-distance(first, p[0]) - distance(second, p[1]), p == (0, 0)))


def comm_kernel(
    circ, across, ax,
    st, rot, tab, adv, modes,
    S, W, GA, GC, KG, CS, conv, E, MB, XR, PS, R, MA, RA, T,
    rotor, load_sem, tab_sem, rot_sem, ga_send, ga_recv, gc_send, gc_recv,
    x_send, x_recv, a_send, a_recv, m_send, m_recv,
):
    r, c, y = lax.axis_index("row"), lax.axis_index("circ"), lax.axis_index("ax")
    na, nt = S.shape[1] - 2, S.shape[2]
    last = ax - 1
    load = pltpu.make_async_copy(st.at[0], S.at[:, pl.ds(1, na)], load_sem)
    load.start()
    table = pltpu.make_async_copy(tab.at[c], E, tab_sem)
    table.start()
    turn = pltpu.make_async_copy(rot, rotor, rot_sem)
    turn.start()

    along = circ // across
    lines = [lax.rem(y + d, ax) for d in range(ax)]
    layers = [lax.rem(c // across + d, along) * across for d in range(along)]
    columns = [lax.rem(lax.rem(c, across) + d, across) for d in range(across)]
    near_offsets, far_offsets = offsets(ax, 2), offsets(along, across)

    def near(i):
        d, e = near_offsets[i]
        return (1 - r if e else r, c, lines[d])

    def sector(i):
        d, e = far_offsets[i]
        return layers[d] + columns[e]

    def far(i):
        return (1 - r, sector(i), y)

    right, left = (r, lax.rem(c + 1, circ), y), (r, lax.rem(c + circ - 1, circ), y)
    barrier = pltpu.get_barrier_semaphore()

    def greet(device):
        pl.semaphore_signal(barrier, inc=1, device_id=device, device_id_type=MESH)

    def loop(lo, hi, body):
        def step(i, carry):
            body(i)
            return carry

        lax.fori_loop(lo, hi, step, 0)

    for i in range(circ // 2):
        greet(far(i))
    for i in range(2 * ax - 1):
        greet(near(i))
    for i in range(circ // 2, circ - 1):
        greet(far(i))
    greet(right)
    greet(left)

    load.wait()

    def speeds(a, fastest):
        q = [S[f, a] for f in range(FIELDS)]
        w, inverse = primitive(q)
        for i in range(4):
            W[i, a] = w[i]
        speed = jnp.maximum(jnp.maximum(jnp.abs(w[0]), jnp.abs(w[1])), jnp.abs(w[2]))
        speed = speed + jnp.sqrt(1.4 * w[3] * inverse)
        for i in range(nt // 8):
            fastest = jnp.maximum(fastest, speed[8 * i : 8 * i + 8])
        return fastest

    MA[...] = jnp.max(lax.fori_loop(1, na + 1, speeds, jnp.zeros((8, 128), F32)), axis=0, keepdims=True)
    for f in range(FIELDS):
        CS[0, f] = S[f, 1 : na + 1, nt - 1]
        CS[1, f] = S[f, 1 : na + 1, 0]

    lane = lax.broadcasted_iota(jnp.int32, (nt, 128), 1)
    cell = lax.broadcasted_iota(jnp.int32, (nt, 128), 0)
    edge = lax.broadcasted_iota(jnp.int32, (8, 128), 0)

    def inside_next(v):
        return jnp.where(cell == nt - 1, 0.0, pltpu.roll(v, nt - 1, 0))

    def inside_prev(v):
        return jnp.where(cell == 0, 0.0, pltpu.roll(v, 1, 0))

    def plane(a):
        q, w = [S[f, a] for f in range(FIELDS)], [W[i, a] for i in range(4)]
        qu, wu = [S[f, a + 1] for f in range(FIELDS)], [W[i, a + 1] for i in range(4)]
        qd, wd = [S[f, a - 1] for f in range(FIELDS)], [W[i, a - 1] for i in range(4)]
        for f in range(FIELDS):
            qf = q[f]
            smooth = qu[f] + qd[f] - 6.0 * qf + lanes_next(qf, lane) + lanes_prev(qf, lane)
            adv[0, f, a - 1] = qf + SMOOTH * (smooth + inside_next(qf) + inside_prev(qf))
            f1, f2 = flux(q, w, 1, f), flux(q, w, 2, f)
            moved = flux(qu, wu, 0, f) - flux(qd, wd, 0, f)
            moved = moved + lanes_next(f2, lane) - lanes_prev(f2, lane)
            conv[f, a - 1] = 0.5 * (moved + inside_next(f1) - inside_prev(f1))

    for a in (0, na + 1):
        for f in range(FIELDS):
            S[f, a] = jnp.zeros((nt, 128), F32)
        for i in range(4):
            W[i, a] = jnp.zeros((nt, 128), F32)

    band = 128 // ax

    @pl.when(y == last)
    def _():
        q = [S[f, na] for f in range(FIELDS)]
        w = [W[i, na] for i in range(4)]
        qm = [S[f, na - 1] for f in range(FIELDS)]
        wm = [W[i, na - 1] for i in range(4)]
        group = lax.broadcasted_iota(jnp.int32, (ROWS, 128), 1) // band
        quarter = group[:8] // 2
        terms = [[], []]

        for f in range(FIELDS):
            qf = q[f]
            smooth = qm[f] - 5.0 * qf + lanes_next(qf, lane) + lanes_prev(qf, lane)
            smooth = smooth + inside_next(qf) + inside_prev(qf)
            still = qf + SMOOTH * smooth
            f1, f2 = flux(q, w, 1, f), flux(q, w, 2, f)
            moved = flux(q, w, 0, f) - flux(qm, wm, 0, f)
            moved = moved + lanes_next(f2, lane) - lanes_prev(f2, lane)
            moved = 0.5 * (moved + inside_next(f1) - inside_prev(f1))
            q_ends = jnp.where(edge == 0, qf[nt - 1 : nt], jnp.where(edge == 1, qf[0:1], 0.0))
            f_ends = jnp.where(edge == 0, -f1[nt - 1 : nt], jnp.where(edge == 1, f1[0:1], 0.0))
            for part, (inner, ends) in enumerate(((still, SMOOTH * q_ends), (moved, 0.5 * f_ends))):
                whole = jnp.concatenate([inner, ends], axis=0)
                terms[part].append(whole)
        terms = terms[0] + terms[1]
        placed = [pltpu.roll(v, band * g, 1) if g else v for g, v in enumerate(terms[:8])]
        others = [terms[8], pltpu.roll(terms[9], band, 1)]
        for k in range(ax):
            chosen = placed[0]
            for g in range(1, 8):
                chosen = jnp.where(group == (g + k) % ax, placed[g], chosen)
            chosen = pltpu.roll(chosen, 128 - band * k, 1) if k else chosen
            rest = jnp.where(group == k, others[0], others[1])
            turned = [pltpu.roll(rest[8 * i : 8 * i + 8], (32 * i - band * k) % 128, 1) for i in range(5)]
            MB[k, : ROWS - 8] = chosen[: ROWS - 8]
            MB[k, ROWS - 8 : ROWS] = jnp.where(edge < 2, chosen[ROWS - 8 :], pltpu.roll(turned[4], 2, 0))
            for i in range(1, 4):
                turned[0] = jnp.where(quarter == i, turned[i], turned[0])
            MB[k, ROWS:] = turned[0]
        XR[...] = MB[last]

    loop(1, 1 + EARLY, plane)
    pl.semaphore_wait(barrier, 2 * ax - 1 + circ - 1 + 2)

    def send(src, dst, sent, got, device):
        return pltpu.make_async_remote_copy(
            src_ref=src, dst_ref=dst, send_sem=sent, recv_sem=got, device_id=device, device_id_type=MESH
        )

    def drain(ref, sem):
        pltpu.make_async_copy(ref, ref, sem).wait()

    @pl.when(y == last)
    def _():
        for k in sorted(range(last), key=lambda k: -distance(ax, last - k)):
            send(MB.at[k], XR, x_send, x_recv, (r, c, k)).start()

    for i in range(2 * ax - 1):
        send(MA, RA.at[i], a_send, a_recv, near(i)).start()

    gc_right = send(CS.at[0], GC.at[0], gc_send.at[0], gc_recv.at[0], right)
    gc_left = send(CS.at[1], GC.at[1], gc_send.at[1], gc_recv.at[1], left)
    gc_right.start()
    gc_left.start()
    ga_up = send(S.at[:, na], GA.at[0], ga_send.at[0], ga_recv.at[0], (r, c, lax.rem(y + 1, ax)))
    ga_down = send(S.at[:, 1], GA.at[1], ga_send.at[1], ga_recv.at[1], (r, c, lax.rem(y + last, ax)))

    loop(1 + EARLY, na + 1, plane)
    drain(RA.at[pl.ds(0, 2 * ax - 1)], a_recv)
    fastest = jnp.max(lax.fori_loop(0, 2 * ax - 1, lambda i, m: jnp.maximum(m, RA[i]), MA[...]))

    table.wait()

    @pl.when(y != last)
    def _():
        drain(XR, x_recv)

    def split(v):
        high = v.astype(jnp.bfloat16).astype(F32)
        parts = [high, v - high, high, jnp.zeros((DEPTH - 3 * ROWS, 128), F32)]
        return jnp.concatenate(parts, axis=0).astype(jnp.bfloat16)

    packed = XR[ROWS:]
    rest = [pltpu.roll(packed, 128 - 32 * i, 1) if i else packed for i in range(4)]
    rest = jnp.concatenate(rest + [pltpu.roll(XR[ROWS - 8 : ROWS], 6, 0)], axis=0)
    rest = jnp.where(lax.broadcasted_iota(jnp.int32, (ROWS, 128), 1) < 32, rest, 0.0)
    factors = E[...].reshape(circ, 8, DEPTH)

    def dot(i, v):
        rows = pltpu.roll(factors, 8 - 2 * i, 1) if i else factors
        rows = rows.reshape(circ * 8, DEPTH).astype(jnp.bfloat16)
        return jnp.dot(rows, v, preferred_element_type=F32).reshape(circ, 8, 128)

    PS[:, 0:8] = dot(0, split(XR[:ROWS]))
    others = dot(0, split(rest))
    for i in range(1, 4):
        others = others + dot(i, split(pltpu.roll(rest, 32 * i, 1)))
    PS[:, 8:16] = jnp.where(lax.broadcasted_iota(jnp.int32, (circ, 8, 128), 1) == 2, fastest, others)

    for i in range(circ):
        share = pl.ds(0, SENT)
        send(PS.at[sector(i), share], R.at[i, share], m_send, m_recv, far(i)).start()

    ga_up.start()
    ga_down.start()

    turn.wait()
    mode = c * MODES_HERE + edge // 2
    total = circ * nt
    angle = ((mode * rotor[0, 0]) & (total - 1)).astype(F32) * (2.0 * math.pi / total)
    imaginary = lax.rem(edge, 2) == 1
    orient = (2 * r - 1).astype(F32)
    cosine = jnp.cos(angle)
    sine = jnp.where(imaginary, orient, -orient) * jnp.sin(angle)

    ga_up.wait_recv()
    ga_down.wait_recv()
    for side, a, sign, alone in ((0, 0, -0.5, y == 0), (1, na - 1, 0.5, y == last)):
        ghost = [jnp.where(alone, S[f, a + 1], GA[side, f]) for f in range(FIELDS)]
        w, _ = primitive(ghost)
        for f in range(FIELDS):
            adv[0, f, a] = adv[0, f, a] + SMOOTH * ghost[f]
            conv[f, a] = conv[f, a] + sign * flux(ghost, w, 0, f)
    gc_right.wait_recv()
    gc_left.wait_recv()

    drain(R.at[:, pl.ds(0, SENT)], m_recv)
    speed_row = lax.broadcasted_iota(jnp.int32, (SENT - 8, 128), 0) == 2

    def gather(i, sums):
        tail = R[i, 8:SENT]
        return sums[0] + R[i, 0:8], jnp.where(speed_row, jnp.maximum(sums[1], tail), sums[1] + tail)

    sums, tail = lax.fori_loop(1, circ, gather, (R[0, 0:8], R[0, 8:SENT]))
    T[...] = jnp.zeros((8, 128), F32)
    T[0 : SENT - 8] = tail
    step = 0.8 / (3.0 * jnp.full((8, 128), jnp.max(T[2:3]), F32))
    step_plane = jnp.concatenate([step] * (nt // 8), axis=0)

    for side, sign in ((0, 0.5), (1, -0.5)):
        ghost = [GC[side, f] for f in range(FIELDS)]
        w, _ = primitive(ghost)
        weight = jnp.concatenate([sign * step] * (na // 8), axis=0)
        for f in range(FIELDS):
            KG[side, f] = SMOOTH * ghost[f] + weight * flux(ghost, w, 1, f)

    def finish(a):
        row = pl.ds(a, 1)
        for f in range(FIELDS):
            value = adv[0, f, a] - step_plane * conv[f, a]
            first = jnp.where(edge == 0, KG[0, f, row], 0.0)
            final = jnp.where(edge == 7, KG[1, f, row], 0.0)
            adv[0, f, a, 0:8] = value[0:8] + first
            adv[0, f, a, 8 : nt - 8] = value[8 : nt - 8]
            adv[0, f, a, nt - 8 : nt] = value[nt - 8 : nt] + final

    loop(0, na, finish)
    moved = pltpu.roll(sums, 128 - band * FIELDS, 1)
    for i in range(4):
        piece = pltpu.roll(T[...], (band * 3 - 32 * i) % 128, 1)
        piece = pltpu.roll(piece, 2 * i, 0) if i else piece
        moved = jnp.where((edge // 2 == i) & (lane[:8] >= band * 3), piece, moved)
    own = sums - step * moved
    modes[...] = own * cosine + jnp.where(imaginary, pltpu.roll(own, 1, 0), pltpu.roll(own, 7, 0)) * sine

    drain(RA.at[pl.ds(0, 2 * ax - 1)], a_send)
    drain(R.at[:, pl.ds(0, SENT)], m_send)

    @pl.when(y == last)
    def _():
        drain(MB.at[pl.ds(0, last)], x_send)

    for copy in (gc_right, gc_left, ga_up, ga_down):
        copy.wait_send()


def finish_kernel(adv, turned, out, out_modes, modes, sems):
    copies = [pltpu.make_async_copy(adv.at[0, f], out.at[0, f], sems.at[f]) for f in range(FIELDS)]
    for copy in copies:
        copy.start()
    value = turned[...]
    band = modes.shape[-1]
    for f in range(FIELDS):
        here = pltpu.roll(value, 128 - band * f, 1) if f else value
        for i in range(MODES_HERE):
            for part in range(2):
                row = 2 * i + part
                modes[0, i, f, part : part + 1] = here[row : row + 1, :band]
    copies.append(pltpu.make_async_copy(modes, out_modes, sems.at[FIELDS]))
    copies[-1].start()
    for copy in copies:
        copy.wait()


def on_device(circ, ax, state, rotor_step):
    na, nt = state.shape[2], state.shape[3]
    table = jnp.asarray(tables(circ, nt))
    hbm = pl.BlockSpec(memory_space=pltpu.HBM)
    vmem = pl.BlockSpec(memory_space=pltpu.VMEM)
    dma = pltpu.SemaphoreType.DMA
    block = (FIELDS, na, nt, 128)
    adv, turned = pl.pallas_call(
        functools.partial(comm_kernel, circ, 4 if circ % 4 == 0 else 1, ax),
        out_shape=[pltpu.VMEM(state.shape, F32), pltpu.VMEM((8, 128), F32)],
        in_specs=[hbm, hbm, hbm],
        out_specs=[vmem, vmem],
        scratch_shapes=[
            pltpu.VMEM((FIELDS, na + 2, nt, 128), F32),
            pltpu.VMEM((4, na + 2, nt, 128), F32),
            pltpu.VMEM((2, FIELDS, nt, 128), F32),
            pltpu.VMEM((2, FIELDS, na, 128), F32),
            pltpu.VMEM((2, FIELDS, na, 128), F32),
            pltpu.VMEM((2, FIELDS, na, 128), F32),
            pltpu.VMEM(block, F32),
            pltpu.VMEM((circ * 8, DEPTH), F32),
            pltpu.VMEM((ax, BAND_ROWS, 128), F32),
            pltpu.VMEM((BAND_ROWS, 128), F32),
            pltpu.VMEM((circ, 16, 128), F32),
            pltpu.VMEM((circ, 16, 128), F32),
            pltpu.VMEM((1, 128), F32),
            pltpu.VMEM((2 * ax, 1, 128), F32),
            pltpu.VMEM((8, 128), F32),
            pltpu.SMEM((1, 1), jnp.int32),
            dma, dma, dma, dma((2,)), dma((2,)), dma((2,)), dma((2,)),
            dma, dma, dma, dma, dma, dma,
        ],
        compiler_params=pltpu.CompilerParams(
            collective_id=0, has_side_effects=True, vmem_limit_bytes=56 * 2**20
        ),
        name="exchange",
    )(state, rotor_step.reshape(1, 1), table)
    return pl.pallas_call(
        finish_kernel,
        out_shape=[
            jax.ShapeDtypeStruct(state.shape, F32),
            jax.ShapeDtypeStruct((1, MODES_HERE, FIELDS, 2, 128 // ax), F32),
        ],
        in_specs=[vmem, vmem],
        out_specs=[hbm, hbm],
        scratch_shapes=[pltpu.VMEM((1, MODES_HERE, FIELDS, 2, 128 // ax), F32), dma((FIELDS + 1,))],
        compiler_params=pltpu.CompilerParams(vmem_limit_bytes=16 * 2**20),
        name="finish",
    )(pltpu.with_memory_space_constraint(adv, pltpu.VMEM), pltpu.with_memory_space_constraint(turned, pltpu.VMEM))


def solution(mesh):
    return jax.shard_map(
        functools.partial(on_device, mesh.shape["circ"], mesh.shape["ax"]),
        mesh=mesh,
        in_specs=(P("row", None, "ax", "circ", None), P()),
        out_specs=(P("row", None, "ax", "circ", None), P("row", "circ", None, None, "ax")),
        check_vma=False,
    )
```

```python
import functools
import math

import jax
import jax.numpy as jnp
import numpy as np
from jax import lax
from jax.experimental import pallas as pl
from jax.experimental.pallas import tpu as pltpu
from jax.sharding import PartitionSpec as P

MESH = pl.DeviceIdType.MESH
F32 = jnp.float32
FIELDS = 5
MODES_HERE = 4
ROWS = 40
DEPTH = 128
BAND_ROWS = 48
SENT = 11
SMOOTH = 0.8 / 6.0
EARLY = 0


def tables(circ, cells):
    total = circ * cells
    sector = np.arange(circ)[:, None]
    position = np.zeros((circ, ROWS), np.int64)
    position[:, :cells] = sector * cells + np.arange(cells)[None]
    position[:, cells] = sector[:, 0] * cells + cells
    position[:, cells + 1] = sector[:, 0] * cells - 1
    valid = np.arange(ROWS) < cells + 2
    owner, inner, part = np.meshgrid(np.arange(circ), np.arange(MODES_HERE), np.arange(2), indexing="ij")
    mode = (owner * MODES_HERE + inner).reshape(-1)
    part = part.reshape(-1)
    phase = (mode[None, :, None] * position[:, None, :]) % total
    angle = phase * (2.0 * math.pi / total)
    value = np.where(part[None, :, None] == 0, np.cos(angle), -np.sin(angle)) * math.sqrt(2.0 / total)
    value = np.where(valid[None, None], value, 0.0).astype(np.float32)
    high = value.astype(jnp.bfloat16).astype(np.float32)
    low = (value - high).astype(jnp.bfloat16).astype(np.float32)
    rest = np.zeros((circ, value.shape[1], DEPTH - 3 * ROWS), np.float32)
    return np.concatenate([high, high, low, rest], axis=2)


def flux(q, w, d, f):
    value = q[f] * w[d]
    if f == 1 + d:
        value = value + w[3]
    if f == 4:
        value = value + w[3] * w[d]
    return value


def primitive(q):
    inverse = 1.0 / q[0]
    u = [q[1 + d] * inverse for d in range(3)]
    p = 0.4 * (q[4] - 0.5 * (q[1] * u[0] + q[2] * u[1] + q[3] * u[2]))
    return u + [p], inverse


def lanes_next(v, lane):
    return jnp.where(lane == 127, v, pltpu.roll(v, 127, 1))


def lanes_prev(v, lane):
    return jnp.where(lane == 0, v, pltpu.roll(v, 1, 1))


def distance(n, d):
    return min(d, n - d)


def offsets(first, second):
    pairs = [(d, e) for d in range(first) for e in range(second)]
    return sorted(pairs, key=lambda p: (-distance(first, p[0]) - distance(second, p[1]), p == (0, 0)))


def comm_kernel(
    circ, across, ax,
    st, rot, tab, base, conv, R, turns,
    S, W, GA, GC, CS, E, MB, XR, PS, MA, RA,
    rotor, load_sem, tab_sem, rot_sem, ga_send, ga_recv, gc_send, gc_recv,
    x_send, x_recv, a_send, a_recv, m_send, m_recv,
):
    r, c, y = lax.axis_index("row"), lax.axis_index("circ"), lax.axis_index("ax")
    na, nt = S.shape[1] - 2, S.shape[2]
    last = ax - 1
    load = pltpu.make_async_copy(st.at[0], S.at[:, pl.ds(1, na)], load_sem)
    load.start()
    table = pltpu.make_async_copy(tab.at[c], E, tab_sem)
    table.start()
    turn = pltpu.make_async_copy(rot, rotor, rot_sem)
    turn.start()

    along = circ // across
    lines = [lax.rem(y + d, ax) for d in range(ax)]
    layers = [lax.rem(c // across + d, along) * across for d in range(along)]
    columns = [lax.rem(lax.rem(c, across) + d, across) for d in range(across)]
    near_offsets, far_offsets = offsets(ax, 2), offsets(along, across)

    def near(i):
        d, e = near_offsets[i]
        return (1 - r if e else r, c, lines[d])

    def sector(i):
        d, e = far_offsets[i]
        return layers[d] + columns[e]

    def far(i):
        return (1 - r, sector(i), y)

    right, left = (r, lax.rem(c + 1, circ), y), (r, lax.rem(c + circ - 1, circ), y)
    barrier = pltpu.get_barrier_semaphore()

    def greet(device):
        pl.semaphore_signal(barrier, inc=1, device_id=device, device_id_type=MESH)

    def loop(lo, hi, body):
        def step(i, carry):
            body(i)
            return carry

        lax.fori_loop(lo, hi, step, 0)

    for i in range(circ // 2):
        greet(far(i))
    for i in range(2 * ax - 1):
        greet(near(i))
    for i in range(circ // 2, circ - 1):
        greet(far(i))
    greet(right)
    greet(left)

    load.wait()

    def speeds(a, fastest):
        q = [S[f, a] for f in range(FIELDS)]
        w, inverse = primitive(q)
        for i in range(4):
            W[i, a] = w[i]
        speed = jnp.maximum(jnp.maximum(jnp.abs(w[0]), jnp.abs(w[1])), jnp.abs(w[2]))
        speed = speed + jnp.sqrt(1.4 * w[3] * inverse)
        for i in range(nt // 8):
            fastest = jnp.maximum(fastest, speed[8 * i : 8 * i + 8])
        return fastest

    MA[...] = jnp.max(lax.fori_loop(1, na + 1, speeds, jnp.zeros((8, 128), F32)), axis=0, keepdims=True)
    for f in range(FIELDS):
        CS[0, f] = S[f, 1 : na + 1, nt - 1]
        CS[1, f] = S[f, 1 : na + 1, 0]

    lane = lax.broadcasted_iota(jnp.int32, (nt, 128), 1)
    cell = lax.broadcasted_iota(jnp.int32, (nt, 128), 0)
    edge = lax.broadcasted_iota(jnp.int32, (8, 128), 0)

    def inside_next(v):
        return jnp.where(cell == nt - 1, 0.0, pltpu.roll(v, nt - 1, 0))

    def inside_prev(v):
        return jnp.where(cell == 0, 0.0, pltpu.roll(v, 1, 0))

    def plane(a):
        q, w = [S[f, a] for f in range(FIELDS)], [W[i, a] for i in range(4)]
        qu, wu = [S[f, a + 1] for f in range(FIELDS)], [W[i, a + 1] for i in range(4)]
        qd, wd = [S[f, a - 1] for f in range(FIELDS)], [W[i, a - 1] for i in range(4)]
        for f in range(FIELDS):
            qf = q[f]
            smooth = qu[f] + qd[f] - 6.0 * qf + lanes_next(qf, lane) + lanes_prev(qf, lane)
            base[f, a - 1] = qf + SMOOTH * (smooth + inside_next(qf) + inside_prev(qf))
            f1, f2 = flux(q, w, 1, f), flux(q, w, 2, f)
            moved = flux(qu, wu, 0, f) - flux(qd, wd, 0, f)
            moved = moved + lanes_next(f2, lane) - lanes_prev(f2, lane)
            conv[f, a - 1] = 0.5 * (moved + inside_next(f1) - inside_prev(f1))

    for a in (0, na + 1):
        for f in range(FIELDS):
            S[f, a] = jnp.zeros((nt, 128), F32)
        for i in range(4):
            W[i, a] = jnp.zeros((nt, 128), F32)

    band = 128 // ax

    @pl.when(y == last)
    def _():
        q = [S[f, na] for f in range(FIELDS)]
        w = [W[i, na] for i in range(4)]
        qm = [S[f, na - 1] for f in range(FIELDS)]
        wm = [W[i, na - 1] for i in range(4)]
        group = lax.broadcasted_iota(jnp.int32, (ROWS, 128), 1) // band
        quarter = group[:8] // 2
        terms = [[], []]

        for f in range(FIELDS):
            qf = q[f]
            smooth = qm[f] - 5.0 * qf + lanes_next(qf, lane) + lanes_prev(qf, lane)
            smooth = smooth + inside_next(qf) + inside_prev(qf)
            still = qf + SMOOTH * smooth
            f1, f2 = flux(q, w, 1, f), flux(q, w, 2, f)
            moved = flux(q, w, 0, f) - flux(qm, wm, 0, f)
            moved = moved + lanes_next(f2, lane) - lanes_prev(f2, lane)
            moved = 0.5 * (moved + inside_next(f1) - inside_prev(f1))
            q_ends = jnp.where(edge == 0, qf[nt - 1 : nt], jnp.where(edge == 1, qf[0:1], 0.0))
            f_ends = jnp.where(edge == 0, -f1[nt - 1 : nt], jnp.where(edge == 1, f1[0:1], 0.0))
            for part, (inner, ends) in enumerate(((still, SMOOTH * q_ends), (moved, 0.5 * f_ends))):
                whole = jnp.concatenate([inner, ends], axis=0)
                terms[part].append(whole)
        terms = terms[0] + terms[1]
        placed = [pltpu.roll(v, band * g, 1) if g else v for g, v in enumerate(terms[:8])]
        others = [terms[8], pltpu.roll(terms[9], band, 1)]
        for k in range(ax):
            chosen = placed[0]
            for g in range(1, 8):
                chosen = jnp.where(group == (g + k) % ax, placed[g], chosen)
            chosen = pltpu.roll(chosen, 128 - band * k, 1) if k else chosen
            rest = jnp.where(group == k, others[0], others[1])
            turned = [pltpu.roll(rest[8 * i : 8 * i + 8], (32 * i - band * k) % 128, 1) for i in range(5)]
            MB[k, : ROWS - 8] = chosen[: ROWS - 8]
            MB[k, ROWS - 8 : ROWS] = jnp.where(edge < 2, chosen[ROWS - 8 :], pltpu.roll(turned[4], 2, 0))
            for i in range(1, 4):
                turned[0] = jnp.where(quarter == i, turned[i], turned[0])
            MB[k, ROWS:] = turned[0]
        XR[...] = MB[last]

    loop(1, 1 + EARLY, plane)
    pl.semaphore_wait(barrier, 2 * ax - 1 + circ - 1 + 2)

    def send(src, dst, sent, got, device):
        return pltpu.make_async_remote_copy(
            src_ref=src, dst_ref=dst, send_sem=sent, recv_sem=got, device_id=device, device_id_type=MESH
        )

    def drain(ref, sem):
        pltpu.make_async_copy(ref, ref, sem).wait()

    @pl.when(y == last)
    def _():
        for k in sorted(range(last), key=lambda k: -distance(ax, last - k)):
            send(MB.at[k], XR, x_send, x_recv, (r, c, k)).start()

    for i in range(2 * ax - 1):
        send(MA, RA.at[i], a_send, a_recv, near(i)).start()

    gc_right = send(CS.at[0], GC.at[0], gc_send.at[0], gc_recv.at[0], right)
    gc_left = send(CS.at[1], GC.at[1], gc_send.at[1], gc_recv.at[1], left)
    gc_right.start()
    gc_left.start()
    ga_up = send(S.at[:, na], GA.at[0], ga_send.at[0], ga_recv.at[0], (r, c, lax.rem(y + 1, ax)))
    ga_down = send(S.at[:, 1], GA.at[1], ga_send.at[1], ga_recv.at[1], (r, c, lax.rem(y + last, ax)))

    loop(1 + EARLY, na + 1, plane)
    drain(RA.at[pl.ds(0, 2 * ax - 1)], a_recv)
    fastest = jnp.max(lax.fori_loop(0, 2 * ax - 1, lambda i, m: jnp.maximum(m, RA[i]), MA[...]))

    table.wait()

    @pl.when(y != last)
    def _():
        drain(XR, x_recv)

    def split(v):
        high = v.astype(jnp.bfloat16).astype(F32)
        parts = [high, v - high, high, jnp.zeros((DEPTH - 3 * ROWS, 128), F32)]
        return jnp.concatenate(parts, axis=0).astype(jnp.bfloat16)

    packed = XR[ROWS:]
    rest = [pltpu.roll(packed, 128 - 32 * i, 1) if i else packed for i in range(4)]
    rest = jnp.concatenate(rest + [pltpu.roll(XR[ROWS - 8 : ROWS], 6, 0)], axis=0)
    rest = jnp.where(lax.broadcasted_iota(jnp.int32, (ROWS, 128), 1) < 32, rest, 0.0)
    factors = E[...].reshape(circ, 8, DEPTH)

    def dot(i, v):
        rows = pltpu.roll(factors, 8 - 2 * i, 1) if i else factors
        rows = rows.reshape(circ * 8, DEPTH).astype(jnp.bfloat16)
        return jnp.dot(rows, v, preferred_element_type=F32).reshape(circ, 8, 128)

    PS[:, 0:8] = dot(0, split(XR[:ROWS]))
    others = dot(0, split(rest))
    for i in range(1, 4):
        others = others + dot(i, split(pltpu.roll(rest, 32 * i, 1)))
    PS[:, 8:16] = jnp.where(lax.broadcasted_iota(jnp.int32, (circ, 8, 128), 1) == 2, fastest, others)

    for i in range(circ):
        share = pl.ds(0, SENT)
        send(PS.at[i, share], R.at[c, share], m_send, m_recv, (1 - r, i, y)).start()

    ga_up.start()
    ga_down.start()

    turn.wait()
    mode = c * MODES_HERE + edge // 2
    total = circ * nt
    angle = ((mode * rotor[0, 0]) & (total - 1)).astype(F32) * (2.0 * math.pi / total)
    imaginary = lax.rem(edge, 2) == 1
    orient = (2 * r - 1).astype(F32)
    turns[0] = jnp.cos(angle)
    turns[1] = jnp.where(imaginary, orient, -orient) * jnp.sin(angle)

    ga_up.wait_recv()
    ga_down.wait_recv()
    for side, a, sign, alone in ((0, 0, -0.5, y == 0), (1, na - 1, 0.5, y == last)):
        ghost = [jnp.where(alone, S[f, a + 1], GA[side, f]) for f in range(FIELDS)]
        w, _ = primitive(ghost)
        for f in range(FIELDS):
            base[f, a] = base[f, a] + SMOOTH * ghost[f]
            conv[f, a] = conv[f, a] + sign * flux(ghost, w, 0, f)
    for copy in (gc_right, gc_left):
        copy.wait_send()
        copy.wait_recv()

    for side, at, row, sign in ((0, 0, 0, -0.5), (1, nt - 8, 7, 0.5)):
        ghost = [GC[side, f] for f in range(FIELDS)]
        w, _ = primitive(ghost)
        for f in range(FIELDS):
            GC[side, f] = SMOOTH * ghost[f]
            CS[side, f] = sign * flux(ghost, w, 1, f)

        def ghosts(a, side=side, at=at, row=row):
            here, rows = pl.ds(a, 1), pl.ds(at, 8)
            for f in range(FIELDS):
                base[f, a, rows] = base[f, a, rows] + jnp.where(edge == row, GC[side, f, here], 0.0)
                conv[f, a, rows] = conv[f, a, rows] + jnp.where(edge == row, CS[side, f, here], 0.0)

        loop(0, na, ghosts)

    drain(RA.at[pl.ds(0, 2 * ax - 1)], a_send)

    @pl.when(y == last)
    def _():
        drain(MB.at[pl.ds(0, last)], x_send)

    ga_up.wait_send()
    ga_down.wait_send()
    drain(R.at[:, pl.ds(0, SENT)], m_send)
    drain(R.at[:, pl.ds(0, SENT)], m_recv)


def finish_kernel(base, conv, R, turns, out, out_modes, adv, modes, sems):
    circ, na, nt = R.shape[0], base.shape[1], base.shape[2]
    band = modes.shape[-1]
    lane = lax.broadcasted_iota(jnp.int32, (8, 128), 1)
    edge = lax.broadcasted_iota(jnp.int32, (8, 128), 0)

    fastest = R[0, SENT - 1 : SENT]
    for i in range(1, circ):
        fastest = jnp.maximum(fastest, R[i, SENT - 1 : SENT])
    step = 0.8 / (3.0 * jnp.broadcast_to(fastest, (nt, 128)))
    copies = []
    for f in range(FIELDS):
        for a in range(na):
            adv[f, a] = base[f, a] - step * conv[f, a]
        copies.append(pltpu.make_async_copy(adv.at[f], out.at[0, f], sems.at[f]))
        copies[-1].start()

    sums, tail = R[0, 0:8], R[0, 8 : SENT - 1]
    for i in range(1, circ):
        sums, tail = sums + R[i, 0:8], tail + R[i, 8 : SENT - 1]
    tail = jnp.concatenate([tail, jnp.zeros((17 - SENT, 128), F32)], axis=0)
    moved = pltpu.roll(sums, 128 - band * FIELDS, 1)
    for i in range(4):
        piece = pltpu.roll(tail, (band * 3 - 32 * i) % 128, 1)
        piece = pltpu.roll(piece, 2 * i, 0) if i else piece
        moved = jnp.where((edge // 2 == i) & (lane >= band * 3), piece, moved)
    own = sums - step[:8] * moved
    other = jnp.where(lax.rem(edge, 2) == 1, pltpu.roll(own, 1, 0), pltpu.roll(own, 7, 0))
    value = own * turns[0] + other * turns[1]
    for f in range(FIELDS):
        here = pltpu.roll(value, 128 - band * f, 1) if f else value
        for i in range(MODES_HERE):
            for part in range(2):
                row = 2 * i + part
                modes[0, i, f, part : part + 1] = here[row : row + 1, :band]
    copies.append(pltpu.make_async_copy(modes, out_modes, sems.at[FIELDS]))
    copies[-1].start()
    for copy in copies:
        copy.wait()


def on_device(circ, ax, state, rotor_step):
    na, nt = state.shape[2], state.shape[3]
    table = jnp.asarray(tables(circ, nt))
    hbm = pl.BlockSpec(memory_space=pltpu.HBM)
    vmem = pl.BlockSpec(memory_space=pltpu.VMEM)
    dma = pltpu.SemaphoreType.DMA
    block = (FIELDS, na, nt, 128)
    results = pl.pallas_call(
        functools.partial(comm_kernel, circ, 4 if circ % 4 == 0 else 1, ax),
        out_shape=[
            pltpu.VMEM(block, F32),
            pltpu.VMEM(block, F32),
            pltpu.VMEM((circ, 16, 128), F32),
            pltpu.VMEM((2, 8, 128), F32),
        ],
        in_specs=[hbm, hbm, hbm],
        out_specs=[vmem] * 4,
        scratch_shapes=[
            pltpu.VMEM((FIELDS, na + 2, nt, 128), F32),
            pltpu.VMEM((4, na + 2, nt, 128), F32),
            pltpu.VMEM((2, FIELDS, nt, 128), F32),
            pltpu.VMEM((2, FIELDS, na, 128), F32),
            pltpu.VMEM((2, FIELDS, na, 128), F32),
            pltpu.VMEM((circ * 8, DEPTH), F32),
            pltpu.VMEM((ax, BAND_ROWS, 128), F32),
            pltpu.VMEM((BAND_ROWS, 128), F32),
            pltpu.VMEM((circ, 16, 128), F32),
            pltpu.VMEM((1, 128), F32),
            pltpu.VMEM((2 * ax, 1, 128), F32),
            pltpu.SMEM((1, 1), jnp.int32),
            dma, dma, dma, dma((2,)), dma((2,)), dma((2,)), dma((2,)),
            dma, dma, dma, dma, dma, dma,
        ],
        compiler_params=pltpu.CompilerParams(
            collective_id=0, has_side_effects=True, vmem_limit_bytes=56 * 2**20
        ),
        name="exchange",
    )(state, rotor_step.reshape(1, 1), table)
    return pl.pallas_call(
        finish_kernel,
        out_shape=[
            jax.ShapeDtypeStruct(state.shape, F32),
            jax.ShapeDtypeStruct((1, MODES_HERE, FIELDS, 2, 128 // ax), F32),
        ],
        in_specs=[vmem] * 4,
        out_specs=[hbm, hbm],
        scratch_shapes=[
            pltpu.VMEM(block, F32),
            pltpu.VMEM((1, MODES_HERE, FIELDS, 2, 128 // ax), F32),
            dma((FIELDS + 1,)),
        ],
        compiler_params=pltpu.CompilerParams(vmem_limit_bytes=16 * 2**20),
        name="finish",
    )(*(pltpu.with_memory_space_constraint(v, pltpu.VMEM) for v in results))


def solution(mesh):
    return jax.shard_map(
        functools.partial(on_device, mesh.shape["circ"], mesh.shape["ax"]),
        mesh=mesh,
        in_specs=(P("row", None, "ax", "circ", None), P()),
        out_specs=(P("row", None, "ax", "circ", None), P("row", "circ", None, None, "ax")),
        check_vma=False,
    )
```

```python
import functools
import math

import jax
import jax.numpy as jnp
import numpy as np
from jax import lax
from jax.experimental import pallas as pl
from jax.experimental.pallas import tpu as pltpu
from jax.sharding import PartitionSpec as P

MESH = pl.DeviceIdType.MESH
F32 = jnp.float32
FIELDS = 5
MODES_HERE = 4
ROWS = 40
DEPTH = 128
BAND_ROWS = 48
SENT = 11
SMOOTH = 0.8 / 6.0


def tables(circ, cells):
    total = circ * cells
    sector = np.arange(circ)[:, None]
    position = np.zeros((circ, ROWS), np.int64)
    position[:, :cells] = sector * cells + np.arange(cells)[None]
    position[:, cells] = sector[:, 0] * cells + cells
    position[:, cells + 1] = sector[:, 0] * cells - 1
    valid = np.arange(ROWS) < cells + 2
    owner, inner, part = np.meshgrid(np.arange(circ), np.arange(MODES_HERE), np.arange(2), indexing="ij")
    mode = (owner * MODES_HERE + inner).reshape(-1)
    part = part.reshape(-1)
    phase = (mode[None, :, None] * position[:, None, :]) % total
    angle = phase * (2.0 * math.pi / total)
    value = np.where(part[None, :, None] == 0, np.cos(angle), -np.sin(angle)) * math.sqrt(2.0 / total)
    value = np.where(valid[None, None], value, 0.0).astype(np.float32)
    high = value.astype(jnp.bfloat16).astype(np.float32)
    low = (value - high).astype(jnp.bfloat16).astype(np.float32)
    rest = np.zeros((circ, value.shape[1], DEPTH - 3 * ROWS), np.float32)
    return np.concatenate([high, high, low, rest], axis=2)


def flux(q, w, d, f):
    value = q[f] * w[d]
    if f == 1 + d:
        value = value + w[3]
    if f == 4:
        value = value + w[3] * w[d]
    return value


def primitive(q):
    inverse = 1.0 / q[0]
    u = [q[1 + d] * inverse for d in range(3)]
    p = 0.4 * (q[4] - 0.5 * (q[1] * u[0] + q[2] * u[1] + q[3] * u[2]))
    return u + [p], inverse


def lanes_next(v, lane):
    return jnp.where(lane == 127, v, pltpu.roll(v, 127, 1))


def lanes_prev(v, lane):
    return jnp.where(lane == 0, v, pltpu.roll(v, 1, 1))


def distance(n, d):
    return min(d, n - d)


def offsets(first, second):
    pairs = [(d, e) for d in range(first) for e in range(second)]
    return sorted(pairs, key=lambda p: (-distance(first, p[0]) - distance(second, p[1]), p == (0, 0)))


def comm_kernel(
    circ, across, ax,
    st, rot, tab, base, conv, R, turns,
    S, W, GA, GC, CS, E, EB, MB, XR, PS, MA, RA,
    rotor, load_sem, tab_sem, rot_sem, ga_send, ga_recv, gc_send, gc_recv,
    x_send, x_recv, a_send, a_recv, m_send, m_recv,
):
    r, c, y = lax.axis_index("row"), lax.axis_index("circ"), lax.axis_index("ax")
    na, nt = S.shape[1] - 2, S.shape[2]
    last = ax - 1
    load = pltpu.make_async_copy(st.at[0], S.at[:, pl.ds(1, na)], load_sem)
    load.start()
    table = pltpu.make_async_copy(tab.at[c], E, tab_sem)
    table.start()
    turn = pltpu.make_async_copy(rot, rotor, rot_sem)
    turn.start()

    lines = [lax.rem(y + d, ax) for d in range(ax)]
    near_offsets, far_offsets = offsets(ax, 2), offsets(circ // across, across)[:-1]
    layers = [lax.rem(c // across + d, circ // across) * across for d in range(circ // across)]
    columns = [lax.rem(lax.rem(c, across) + d, across) for d in range(across)]
    right, left = (r, lax.rem(c + 1, circ), y), (r, lax.rem(c + circ - 1, circ), y)
    up, down = (r, c, lines[1]), (r, c, lines[last])
    barrier = pltpu.get_barrier_semaphore()

    def greet(device):
        pl.semaphore_signal(barrier, inc=1, device_id=device, device_id_type=MESH)

    def loop(lo, hi, body):
        def step(i, carry):
            body(i)
            return carry

        lax.fori_loop(lo, hi, step, 0)

    @pl.when(r == 0)
    def _():
        for device in (up, down, left, right):
            greet(device)
        greet((1, c, y))

    @pl.when(r == 1)
    def _():
        for d, e in near_offsets[:-1]:
            greet((1 - e, c, lines[d]))

    for d, e in far_offsets:
        greet((1, layers[d] + columns[e], y))

    load.wait()

    def speeds(a, fastest):
        q = [S[f, a] for f in range(FIELDS)]
        w, inverse = primitive(q)
        for i in range(4):
            W[i, a] = w[i]
        speed = jnp.maximum(jnp.maximum(jnp.abs(w[0]), jnp.abs(w[1])), jnp.abs(w[2]))
        speed = speed + jnp.sqrt(1.4 * w[3] * inverse)
        for i in range(nt // 8):
            fastest = jnp.maximum(fastest, speed[8 * i : 8 * i + 8])
        return fastest

    MA[...] = jnp.max(lax.fori_loop(1, na + 1, speeds, jnp.zeros((8, 128), F32)), axis=0, keepdims=True)
    for f in range(FIELDS):
        CS[0, f] = S[f, 1 : na + 1, nt - 1]
        CS[1, f] = S[f, 1 : na + 1, 0]

    lane = lax.broadcasted_iota(jnp.int32, (nt, 128), 1)
    cell = lax.broadcasted_iota(jnp.int32, (nt, 128), 0)
    edge = lax.broadcasted_iota(jnp.int32, (8, 128), 0)

    def inside_next(v):
        return jnp.where(cell == nt - 1, 0.0, pltpu.roll(v, nt - 1, 0))

    def inside_prev(v):
        return jnp.where(cell == 0, 0.0, pltpu.roll(v, 1, 0))

    def plane(a):
        q, w = [S[f, a] for f in range(FIELDS)], [W[i, a] for i in range(4)]
        qu, wu = [S[f, a + 1] for f in range(FIELDS)], [W[i, a + 1] for i in range(4)]
        qd, wd = [S[f, a - 1] for f in range(FIELDS)], [W[i, a - 1] for i in range(4)]
        for f in range(FIELDS):
            qf = q[f]
            smooth = qu[f] + qd[f] - 6.0 * qf + lanes_next(qf, lane) + lanes_prev(qf, lane)
            base[f, a - 1] = qf + SMOOTH * (smooth + inside_next(qf) + inside_prev(qf))
            f1, f2 = flux(q, w, 1, f), flux(q, w, 2, f)
            moved = flux(qu, wu, 0, f) - flux(qd, wd, 0, f)
            moved = moved + lanes_next(f2, lane) - lanes_prev(f2, lane)
            conv[f, a - 1] = 0.5 * (moved + inside_next(f1) - inside_prev(f1))

    for a in (0, na + 1):
        for f in range(FIELDS):
            S[f, a] = jnp.zeros((nt, 128), F32)
        for i in range(4):
            W[i, a] = jnp.zeros((nt, 128), F32)

    band = 128 // ax

    @pl.when(y == last)
    def _():
        q = [S[f, na] for f in range(FIELDS)]
        w = [W[i, na] for i in range(4)]
        qm = [S[f, na - 1] for f in range(FIELDS)]
        wm = [W[i, na - 1] for i in range(4)]
        group = lax.broadcasted_iota(jnp.int32, (ROWS, 128), 1) // band
        quarter = group[:8] // 2
        terms = [[], []]

        for f in range(FIELDS):
            qf = q[f]
            smooth = qm[f] - 5.0 * qf + lanes_next(qf, lane) + lanes_prev(qf, lane)
            smooth = smooth + inside_next(qf) + inside_prev(qf)
            still = qf + SMOOTH * smooth
            f1, f2 = flux(q, w, 1, f), flux(q, w, 2, f)
            moved = flux(q, w, 0, f) - flux(qm, wm, 0, f)
            moved = moved + lanes_next(f2, lane) - lanes_prev(f2, lane)
            moved = 0.5 * (moved + inside_next(f1) - inside_prev(f1))
            q_ends = jnp.where(edge == 0, qf[nt - 1 : nt], jnp.where(edge == 1, qf[0:1], 0.0))
            f_ends = jnp.where(edge == 0, -f1[nt - 1 : nt], jnp.where(edge == 1, f1[0:1], 0.0))
            for part, (inner, ends) in enumerate(((still, SMOOTH * q_ends), (moved, 0.5 * f_ends))):
                whole = jnp.concatenate([inner, ends], axis=0)
                terms[part].append(whole)
        terms = terms[0] + terms[1]
        placed = [pltpu.roll(v, band * g, 1) if g else v for g, v in enumerate(terms[:8])]
        others = [terms[8], pltpu.roll(terms[9], band, 1)]
        for k in range(ax):
            chosen = placed[0]
            for g in range(1, 8):
                chosen = jnp.where(group == (g + k) % ax, placed[g], chosen)
            chosen = pltpu.roll(chosen, 128 - band * k, 1) if k else chosen
            rest = jnp.where(group == k, others[0], others[1])
            turned = [pltpu.roll(rest[8 * i : 8 * i + 8], (32 * i - band * k) % 128, 1) for i in range(5)]
            MB[k, : ROWS - 8] = chosen[: ROWS - 8]
            MB[k, ROWS - 8 : ROWS] = jnp.where(edge < 2, chosen[ROWS - 8 :], pltpu.roll(turned[4], 2, 0))
            for i in range(1, 4):
                turned[0] = jnp.where(quarter == i, turned[i], turned[0])
            MB[k, ROWS:] = turned[0]
        XR[1] = MB[last]

    @pl.when(r == 0)
    def _():
        pl.semaphore_wait(barrier, ax + 4)

    @pl.when(r == 1)
    def _():
        pl.semaphore_wait(barrier, ax - 1 + 2 * circ - 1)

    def send(src, dst, sent, got, device):
        return pltpu.make_async_remote_copy(
            src_ref=src, dst_ref=dst, send_sem=sent, recv_sem=got, device_id=device, device_id_type=MESH
        )

    def drain(ref, sem):
        pltpu.make_async_copy(ref, ref, sem).wait()

    def band_to(k):
        return send(MB.at[k], XR.at[r], x_send, x_recv.at[r], (1, c, k))

    by_distance = sorted(range(ax), key=lambda k: -distance(ax, last - k))

    @pl.when(y == last)
    def _():
        for k in by_distance[:-1]:
            band_to(k).start()

        @pl.when(r == 0)
        def _():
            band_to(last).start()

    def speed_to(i):
        send(MA, RA.at[i], a_send, a_recv, (1, c, lines[near_offsets[i][0]])).start()

    @pl.when(r == 0)
    def _():
        for i in range(2 * ax - 1):
            if near_offsets[i][1]:
                speed_to(i)

    @pl.when(r == 1)
    def _():
        for i in range(2 * ax - 1):
            if not near_offsets[i][1]:
                speed_to(i)

    gc_right = send(CS.at[0], GC.at[0], gc_send.at[0], gc_recv.at[0], right)
    gc_left = send(CS.at[1], GC.at[1], gc_send.at[1], gc_recv.at[1], left)
    gc_right.start()
    gc_left.start()
    ga_up = send(S.at[:, na], GA.at[0], ga_send.at[0], ga_recv.at[0], up)
    ga_down = send(S.at[:, 1], GA.at[1], ga_send.at[1], ga_recv.at[1], down)

    loop(1, na + 1, plane)
    table.wait()
    factors = E[...].reshape(circ, 8, DEPTH)
    for i in range(4):
        rows = pltpu.roll(factors, 8 - 2 * i, 1) if i else factors
        EB[i] = rows.reshape(circ * 8, DEPTH).astype(jnp.bfloat16)

    sent = pl.ds(0, SENT)

    def split(v):
        high = v.astype(jnp.bfloat16).astype(F32)
        parts = [high, v - high, high, jnp.zeros((DEPTH - 3 * ROWS, 128), F32)]
        return jnp.concatenate(parts, axis=0).astype(jnp.bfloat16)

    def share(i, source):
        device, slot = (1 - source, i, y), lax.rem(c - i + circ, circ)
        return send(PS.at[source, i, sent], R.at[slot, sent], m_send.at[source], m_recv, device)

    @pl.when(r == 1)
    def _():
        drain(XR.at[0], x_recv.at[0])

        @pl.when(y != last)
        def _():
            drain(XR.at[1], x_recv.at[1])

        ga_up.start()
        ga_down.start()
        eight, others = [], []
        for source in range(2):
            packed = XR[source, ROWS:]
            rest = [pltpu.roll(packed, 128 - 32 * i, 1) if i else packed for i in range(4)]
            rest = jnp.concatenate(rest + [pltpu.roll(XR[source, ROWS - 8 : ROWS], 6, 0)], axis=0)
            rest = jnp.where(lax.broadcasted_iota(jnp.int32, (ROWS, 128), 1) < 32, rest, 0.0)
            eight.append(split(XR[source, :ROWS]))
            others.append([split(pltpu.roll(rest, 32 * i, 1) if i else rest) for i in range(4)])

        def dot(i, v):
            return jnp.dot(EB[i], v, preferred_element_type=F32).reshape(circ, 8, v.shape[1])

        first = dot(0, jnp.concatenate(eight, axis=1))
        second = dot(0, jnp.concatenate([others[0][0], others[1][0]], axis=1))
        for i in range(1, 4):
            second = second + dot(i, jnp.concatenate([others[0][i], others[1][i]], axis=1))
        for source in range(2):
            lanes = slice(128 * source, 128 * source + 128)
            PS[source, :, 0:8] = first[:, :, lanes]
            PS[source, :, 8:16] = second[:, :, lanes]
        drain(RA.at[pl.ds(0, 2 * ax - 1)], a_recv)
        fastest = MA[...]
        for i in range(2 * ax - 1):
            fastest = jnp.maximum(fastest, RA[i])
        fastest = jnp.full((1, 128), jnp.max(fastest), F32)
        for source in range(2):
            for i in range(circ):
                PS[source, i, SENT - 1 : SENT] = fastest

        for i in range(circ):
            share(i, 1).start()

            @pl.when(c != i)
            def _(i=i):
                share(i, 0).start()

        R[0] = PS[0, c]

    @pl.when(r == 0)
    def _():
        ga_up.start()
        ga_down.start()


    turn.wait()
    mode = c * MODES_HERE + edge // 2
    total = circ * nt
    angle = ((mode * rotor[0, 0]) & (total - 1)).astype(F32) * (2.0 * math.pi / total)
    imaginary = lax.rem(edge, 2) == 1
    orient = (2 * r - 1).astype(F32)
    turns[0] = jnp.cos(angle)
    turns[1] = jnp.where(imaginary, orient, -orient) * jnp.sin(angle)

    ga_up.wait_recv()
    ga_down.wait_recv()
    for side, a, sign, alone in ((0, 0, -0.5, y == 0), (1, na - 1, 0.5, y == last)):
        ghost = [jnp.where(alone, S[f, a + 1], GA[side, f]) for f in range(FIELDS)]
        w, _ = primitive(ghost)
        for f in range(FIELDS):
            base[f, a] = base[f, a] + SMOOTH * ghost[f]
            conv[f, a] = conv[f, a] + sign * flux(ghost, w, 0, f)
    for copy in (gc_right, gc_left):
        copy.wait_send()
        copy.wait_recv()

    for side, at, row, sign in ((0, 0, 0, -0.5), (1, nt - 8, 7, 0.5)):
        ghost = [GC[side, f] for f in range(FIELDS)]
        w, _ = primitive(ghost)
        for f in range(FIELDS):
            GC[side, f] = SMOOTH * ghost[f]
            CS[side, f] = sign * flux(ghost, w, 1, f)

        def ghosts(a, side=side, at=at, row=row):
            here, rows = pl.ds(a, 1), pl.ds(at, 8)
            for f in range(FIELDS):
                base[f, a, rows] = base[f, a, rows] + jnp.where(edge == row, GC[side, f, here], 0.0)
                conv[f, a, rows] = conv[f, a, rows] + jnp.where(edge == row, CS[side, f, here], 0.0)

        loop(0, na, ghosts)

    ga_up.wait_send()
    ga_down.wait_send()

    @pl.when(r == 0)
    def _():
        drain(RA.at[pl.ds(0, ax)], a_send)

        @pl.when(y == last)
        def _():
            drain(MB, x_send)

        drain(R.at[:, sent], m_recv)

    @pl.when(r == 1)
    def _():
        drain(RA.at[pl.ds(0, ax - 1)], a_send)

        @pl.when(y == last)
        def _():
            drain(MB.at[pl.ds(0, last)], x_send)

        drain(PS.at[0, pl.ds(1, circ - 1), sent], m_send.at[0])
        drain(PS.at[1, :, sent], m_send.at[1])
        drain(R.at[pl.ds(1, circ - 1), sent], m_recv)


def finish_kernel(base, conv, R, turns, out, out_modes, adv, modes, sems):
    circ, na, nt = R.shape[0], base.shape[1], base.shape[2]
    band = modes.shape[-1]
    lane = lax.broadcasted_iota(jnp.int32, (8, 128), 1)
    edge = lax.broadcasted_iota(jnp.int32, (8, 128), 0)

    fastest = R[0, SENT - 1 : SENT]
    for i in range(1, circ):
        fastest = jnp.maximum(fastest, R[i, SENT - 1 : SENT])
    step = 0.8 / (3.0 * jnp.broadcast_to(fastest, (nt, 128)))
    copies = []
    for f in range(FIELDS):
        for a in range(na):
            adv[f, a] = base[f, a] - step * conv[f, a]
        copies.append(pltpu.make_async_copy(adv.at[f], out.at[0, f], sems.at[f]))
        copies[-1].start()

    sums, tail = R[0, 0:8], R[0, 8 : SENT - 1]
    for i in range(1, circ):
        sums, tail = sums + R[i, 0:8], tail + R[i, 8 : SENT - 1]
    tail = jnp.concatenate([tail, jnp.zeros((17 - SENT, 128), F32)], axis=0)
    moved = pltpu.roll(sums, 128 - band * FIELDS, 1)
    for i in range(4):
        piece = pltpu.roll(tail, (band * 3 - 32 * i) % 128, 1)
        piece = pltpu.roll(piece, 2 * i, 0) if i else piece
        moved = jnp.where((edge // 2 == i) & (lane >= band * 3), piece, moved)
    own = sums - step[:8] * moved
    other = jnp.where(lax.rem(edge, 2) == 1, pltpu.roll(own, 1, 0), pltpu.roll(own, 7, 0))
    value = own * turns[0] + other * turns[1]
    for f in range(FIELDS):
        here = pltpu.roll(value, 128 - band * f, 1) if f else value
        for i in range(MODES_HERE):
            for part in range(2):
                row = 2 * i + part
                modes[0, i, f, part : part + 1] = here[row : row + 1, :band]
    copies.append(pltpu.make_async_copy(modes, out_modes, sems.at[FIELDS]))
    copies[-1].start()
    for copy in copies:
        copy.wait()


def on_device(circ, ax, state, rotor_step):
    na, nt = state.shape[2], state.shape[3]
    table = jnp.asarray(tables(circ, nt))
    hbm = pl.BlockSpec(memory_space=pltpu.HBM)
    vmem = pl.BlockSpec(memory_space=pltpu.VMEM)
    dma = pltpu.SemaphoreType.DMA
    block = (FIELDS, na, nt, 128)
    results = pl.pallas_call(
        functools.partial(comm_kernel, circ, 4 if circ % 4 == 0 else 1, ax),
        out_shape=[
            pltpu.VMEM(block, F32),
            pltpu.VMEM(block, F32),
            pltpu.VMEM((circ, 16, 128), F32),
            pltpu.VMEM((2, 8, 128), F32),
        ],
        in_specs=[hbm, hbm, hbm],
        out_specs=[vmem] * 4,
        scratch_shapes=[
            pltpu.VMEM((FIELDS, na + 2, nt, 128), F32),
            pltpu.VMEM((4, na + 2, nt, 128), F32),
            pltpu.VMEM((2, FIELDS, nt, 128), F32),
            pltpu.VMEM((2, FIELDS, na, 128), F32),
            pltpu.VMEM((2, FIELDS, na, 128), F32),
            pltpu.VMEM((circ * 8, DEPTH), F32),
            pltpu.VMEM((4, circ * 8, DEPTH), jnp.bfloat16),
            pltpu.VMEM((ax, BAND_ROWS, 128), F32),
            pltpu.VMEM((2, BAND_ROWS, 128), F32),
            pltpu.VMEM((2, circ, 16, 128), F32),
            pltpu.VMEM((1, 128), F32),
            pltpu.VMEM((2 * ax, 1, 128), F32),
            pltpu.SMEM((1, 1), jnp.int32),
            dma, dma, dma, dma((2,)), dma((2,)), dma((2,)), dma((2,)),
            dma, dma((2,)), dma, dma, dma((2,)), dma,
        ],
        compiler_params=pltpu.CompilerParams(
            collective_id=0, has_side_effects=True, vmem_limit_bytes=56 * 2**20
        ),
        name="exchange",
    )(state, rotor_step.reshape(1, 1), table)
    return pl.pallas_call(
        finish_kernel,
        out_shape=[
            jax.ShapeDtypeStruct(state.shape, F32),
            jax.ShapeDtypeStruct((1, MODES_HERE, FIELDS, 2, 128 // ax), F32),
        ],
        in_specs=[vmem] * 4,
        out_specs=[hbm, hbm],
        scratch_shapes=[
            pltpu.VMEM(block, F32),
            pltpu.VMEM((1, MODES_HERE, FIELDS, 2, 128 // ax), F32),
            dma((FIELDS + 1,)),
        ],
        compiler_params=pltpu.CompilerParams(vmem_limit_bytes=16 * 2**20),
        name="finish",
    )(*(pltpu.with_memory_space_constraint(v, pltpu.VMEM) for v in results))


def solution(mesh):
    return jax.shard_map(
        functools.partial(on_device, mesh.shape["circ"], mesh.shape["ax"]),
        mesh=mesh,
        in_specs=(P("row", None, "ax", "circ", None), P()),
        out_specs=(P("row", None, "ax", "circ", None), P("row", "circ", None, None, "ax")),
        check_vma=False,
    )
```

```python
import functools
import math

import jax
import jax.numpy as jnp
import numpy as np
from jax import lax
from jax.experimental import pallas as pl
from jax.experimental.pallas import tpu as pltpu
from jax.sharding import PartitionSpec as P

MESH = pl.DeviceIdType.MESH
F32 = jnp.float32
FIELDS = 5
MODES_HERE = 4
ROWS = 40
DEPTH = 128
BAND_ROWS = 48
SENT = 11
SMOOTH = 0.8 / 6.0


def tables(circ, cells):
    total = circ * cells
    sector = np.arange(circ)[:, None]
    position = np.zeros((circ, ROWS), np.int64)
    position[:, :cells] = sector * cells + np.arange(cells)[None]
    position[:, cells] = sector[:, 0] * cells + cells
    position[:, cells + 1] = sector[:, 0] * cells - 1
    valid = np.arange(ROWS) < cells + 2
    owner, inner, part = np.meshgrid(np.arange(circ), np.arange(MODES_HERE), np.arange(2), indexing="ij")
    mode = (owner * MODES_HERE + inner).reshape(-1)
    part = part.reshape(-1)
    phase = (mode[None, :, None] * position[:, None, :]) % total
    angle = phase * (2.0 * math.pi / total)
    value = np.where(part[None, :, None] == 0, np.cos(angle), -np.sin(angle)) * math.sqrt(2.0 / total)
    value = np.where(valid[None, None], value, 0.0).astype(np.float32)
    high = value.astype(jnp.bfloat16).astype(np.float32)
    low = (value - high).astype(jnp.bfloat16).astype(np.float32)
    rest = np.zeros((circ, value.shape[1], DEPTH - 3 * ROWS), np.float32)
    return np.concatenate([high, high, low, rest], axis=2)


def flux(q, w, d, f):
    value = q[f] * w[d]
    if f == 1 + d:
        value = value + w[3]
    if f == 4:
        value = value + w[3] * w[d]
    return value


def primitive(q):
    inverse = 1.0 / q[0]
    u = [q[1 + d] * inverse for d in range(3)]
    p = 0.4 * (q[4] - 0.5 * (q[1] * u[0] + q[2] * u[1] + q[3] * u[2]))
    return u + [p], inverse


def lanes_next(v, lane):
    return jnp.where(lane == 127, v, pltpu.roll(v, 127, 1))


def lanes_prev(v, lane):
    return jnp.where(lane == 0, v, pltpu.roll(v, 1, 1))


def distance(n, d):
    return min(d, n - d)


def offsets(first, second):
    pairs = [(d, e) for d in range(first) for e in range(second)]
    return sorted(pairs, key=lambda p: (-distance(first, p[0]) - distance(second, p[1]), p == (0, 0)))


def comm_kernel(
    circ, across, ax,
    st, rot, tab, base, conv, R, turns,
    S, W, GA, GC, CS, E, EB, MB, XR, PS, MA, RA,
    rotor, load_sem, tab_sem, rot_sem, ga_send, ga_recv, gc_send, gc_recv,
    x_send, x_recv, a_send, a_recv, m_send, m_recv,
):
    r, c, y = lax.axis_index("row"), lax.axis_index("circ"), lax.axis_index("ax")
    na, nt = S.shape[1] - 2, S.shape[2]
    last = ax - 1
    load = pltpu.make_async_copy(st.at[0], S.at[:, pl.ds(1, na)], load_sem)
    load.start()
    table = pltpu.make_async_copy(tab.at[c], E, tab_sem)
    table.start()
    turn = pltpu.make_async_copy(rot, rotor, rot_sem)
    turn.start()

    lines = [lax.rem(y + d, ax) for d in range(ax)]
    near_offsets, far_offsets = offsets(ax, 2), offsets(circ // across, across)[:-1]
    layers = [lax.rem(c // across + d, circ // across) * across for d in range(circ // across)]
    columns = [lax.rem(lax.rem(c, across) + d, across) for d in range(across)]
    right, left = (r, lax.rem(c + 1, circ), y), (r, lax.rem(c + circ - 1, circ), y)
    up, down = (r, c, lines[1]), (r, c, lines[last])
    barrier = pltpu.get_barrier_semaphore()

    def greet(device):
        pl.semaphore_signal(barrier, inc=1, device_id=device, device_id_type=MESH)

    def loop(lo, hi, body):
        def step(i, carry):
            body(i)
            return carry

        lax.fori_loop(lo, hi, step, 0)

    @pl.when(r == 0)
    def _():
        for device in (up, down, left, right):
            greet(device)
        greet((1, c, y))

    @pl.when(r == 1)
    def _():
        for d, e in near_offsets[:-1]:
            greet((1 - e, c, lines[d]))

    for d, e in far_offsets:
        greet((1, layers[d] + columns[e], y))

    load.wait()

    def speeds(a, fastest):
        q = [S[f, a] for f in range(FIELDS)]
        w, inverse = primitive(q)
        for i in range(4):
            W[i, a] = w[i]
        speed = jnp.maximum(jnp.maximum(jnp.abs(w[0]), jnp.abs(w[1])), jnp.abs(w[2]))
        speed = speed + jnp.sqrt(1.4 * w[3] * inverse)
        for i in range(nt // 8):
            fastest = jnp.maximum(fastest, speed[8 * i : 8 * i + 8])
        return fastest

    MA[...] = jnp.max(lax.fori_loop(1, na + 1, speeds, jnp.zeros((8, 128), F32)), axis=0, keepdims=True)
    for f in range(FIELDS):
        CS[0, f] = S[f, 1 : na + 1, nt - 1]
        CS[1, f] = S[f, 1 : na + 1, 0]

    lane = lax.broadcasted_iota(jnp.int32, (nt, 128), 1)
    cell = lax.broadcasted_iota(jnp.int32, (nt, 128), 0)
    edge = lax.broadcasted_iota(jnp.int32, (8, 128), 0)

    def inside_next(v):
        return jnp.where(cell == nt - 1, 0.0, pltpu.roll(v, nt - 1, 0))

    def inside_prev(v):
        return jnp.where(cell == 0, 0.0, pltpu.roll(v, 1, 0))

    def plane(a):
        q, w = [S[f, a] for f in range(FIELDS)], [W[i, a] for i in range(4)]
        qu, wu = [S[f, a + 1] for f in range(FIELDS)], [W[i, a + 1] for i in range(4)]
        qd, wd = [S[f, a - 1] for f in range(FIELDS)], [W[i, a - 1] for i in range(4)]
        for f in range(FIELDS):
            qf = q[f]
            smooth = qu[f] + qd[f] - 6.0 * qf + lanes_next(qf, lane) + lanes_prev(qf, lane)
            base[f, a - 1] = qf + SMOOTH * (smooth + inside_next(qf) + inside_prev(qf))
            f1, f2 = flux(q, w, 1, f), flux(q, w, 2, f)
            moved = flux(qu, wu, 0, f) - flux(qd, wd, 0, f)
            moved = moved + lanes_next(f2, lane) - lanes_prev(f2, lane)
            conv[f, a - 1] = 0.5 * (moved + inside_next(f1) - inside_prev(f1))

    for a in (0, na + 1):
        for f in range(FIELDS):
            S[f, a] = jnp.zeros((nt, 128), F32)
        for i in range(4):
            W[i, a] = jnp.zeros((nt, 128), F32)

    band = 128 // ax

    @pl.when(y == last)
    def _():
        q = [S[f, na] for f in range(FIELDS)]
        w = [W[i, na] for i in range(4)]
        qm = [S[f, na - 1] for f in range(FIELDS)]
        wm = [W[i, na - 1] for i in range(4)]
        group = lax.broadcasted_iota(jnp.int32, (ROWS, 128), 1) // band
        quarter = group[:8] // 2
        terms = [[], []]

        for f in range(FIELDS):
            qf = q[f]
            smooth = qm[f] - 5.0 * qf + lanes_next(qf, lane) + lanes_prev(qf, lane)
            smooth = smooth + inside_next(qf) + inside_prev(qf)
            still = qf + SMOOTH * smooth
            f1, f2 = flux(q, w, 1, f), flux(q, w, 2, f)
            moved = flux(q, w, 0, f) - flux(qm, wm, 0, f)
            moved = moved + lanes_next(f2, lane) - lanes_prev(f2, lane)
            moved = 0.5 * (moved + inside_next(f1) - inside_prev(f1))
            q_ends = jnp.where(edge == 0, qf[nt - 1 : nt], jnp.where(edge == 1, qf[0:1], 0.0))
            f_ends = jnp.where(edge == 0, -f1[nt - 1 : nt], jnp.where(edge == 1, f1[0:1], 0.0))
            for part, (inner, ends) in enumerate(((still, SMOOTH * q_ends), (moved, 0.5 * f_ends))):
                whole = jnp.concatenate([inner, ends], axis=0)
                terms[part].append(whole)
        terms = terms[0] + terms[1]
        placed = [pltpu.roll(v, band * g, 1) if g else v for g, v in enumerate(terms[:8])]
        others = [terms[8], pltpu.roll(terms[9], band, 1)]
        for k in range(ax):
            chosen = placed[0]
            for g in range(1, 8):
                chosen = jnp.where(group == (g + k) % ax, placed[g], chosen)
            chosen = pltpu.roll(chosen, 128 - band * k, 1) if k else chosen
            rest = jnp.where(group == k, others[0], others[1])
            turned = [pltpu.roll(rest[8 * i : 8 * i + 8], (32 * i - band * k) % 128, 1) for i in range(5)]
            MB[k, : ROWS - 8] = chosen[: ROWS - 8]
            MB[k, ROWS - 8 : ROWS] = jnp.where(edge < 2, chosen[ROWS - 8 :], pltpu.roll(turned[4], 2, 0))
            for i in range(1, 4):
                turned[0] = jnp.where(quarter == i, turned[i], turned[0])
            MB[k, ROWS:] = turned[0]
        XR[1] = MB[last]

    @pl.when(r == 0)
    def _():
        pl.semaphore_wait(barrier, ax + 4)

    @pl.when(r == 1)
    def _():
        pl.semaphore_wait(barrier, ax - 1 + 2 * circ - 1)

    def send(src, dst, sent, got, device):
        return pltpu.make_async_remote_copy(
            src_ref=src, dst_ref=dst, send_sem=sent, recv_sem=got, device_id=device, device_id_type=MESH
        )

    def drain(ref, sem):
        pltpu.make_async_copy(ref, ref, sem).wait()

    def band_to(k):
        return send(MB.at[k], XR.at[r], x_send, x_recv.at[r], (1, c, k))

    by_distance = sorted(range(ax), key=lambda k: (k == last, distance(ax, k)))

    def speed_to(i):
        send(MA, RA.at[i], a_send, a_recv, (1, c, lines[near_offsets[i][0]])).start()

    @pl.when(r == 0)
    def _():
        for i in range(2 * ax - 1):
            if near_offsets[i][1]:
                speed_to(i)

    @pl.when(r == 1)
    def _():
        for i in range(2 * ax - 1):
            if not near_offsets[i][1]:
                speed_to(i)

    @pl.when(y == last)
    def _():
        for k in by_distance[:-1]:
            band_to(k).start()

        @pl.when(r == 0)
        def _():
            band_to(last).start()

    gc_right = send(CS.at[0], GC.at[0], gc_send.at[0], gc_recv.at[0], right)
    gc_left = send(CS.at[1], GC.at[1], gc_send.at[1], gc_recv.at[1], left)
    gc_right.start()
    gc_left.start()
    ga_up = send(S.at[:, na], GA.at[0], ga_send.at[0], ga_recv.at[0], up)
    ga_down = send(S.at[:, 1], GA.at[1], ga_send.at[1], ga_recv.at[1], down)

    loop(1, na + 1, plane)
    table.wait()
    factors = E[...].reshape(circ, 8, DEPTH)
    for i in range(4):
        rows = pltpu.roll(factors, 8 - 2 * i, 1) if i else factors
        EB[i] = rows.reshape(circ * 8, DEPTH).astype(jnp.bfloat16)

    sent = pl.ds(0, SENT)

    def split(v):
        high = v.astype(jnp.bfloat16).astype(F32)
        parts = [high, v - high, high, jnp.zeros((DEPTH - 3 * ROWS, 128), F32)]
        return jnp.concatenate(parts, axis=0).astype(jnp.bfloat16)

    def share(i, source):
        device, slot = (1 - source, i, y), lax.rem(c - i + circ, circ)
        return send(PS.at[source, i, sent], R.at[slot, sent], m_send.at[source], m_recv, device)

    @pl.when(r == 1)
    def _():
        drain(XR.at[0], x_recv.at[0])

        @pl.when(y != last)
        def _():
            drain(XR.at[1], x_recv.at[1])

        ga_up.start()
        ga_down.start()
        eight, others = [], []
        for source in range(2):
            packed = XR[source, ROWS:]
            rest = [pltpu.roll(packed, 128 - 32 * i, 1) if i else packed for i in range(4)]
            rest = jnp.concatenate(rest + [pltpu.roll(XR[source, ROWS - 8 : ROWS], 6, 0)], axis=0)
            rest = jnp.where(lax.broadcasted_iota(jnp.int32, (ROWS, 128), 1) < 32, rest, 0.0)
            eight.append(split(XR[source, :ROWS]))
            others.append([split(pltpu.roll(rest, 32 * i, 1) if i else rest) for i in range(4)])

        def dot(i, v):
            return jnp.dot(EB[i], v, preferred_element_type=F32).reshape(circ, 8, v.shape[1])

        first = dot(0, jnp.concatenate(eight, axis=1))
        second = dot(0, jnp.concatenate([others[0][0], others[1][0]], axis=1))
        for i in range(1, 4):
            second = second + dot(i, jnp.concatenate([others[0][i], others[1][i]], axis=1))
        for source in range(2):
            lanes = slice(128 * source, 128 * source + 128)
            PS[source, :, 0:8] = first[:, :, lanes]
            PS[source, :, 8:16] = second[:, :, lanes]
        drain(RA.at[pl.ds(0, 2 * ax - 1)], a_recv)
        fastest = MA[...]
        for i in range(2 * ax - 1):
            fastest = jnp.maximum(fastest, RA[i])
        fastest = jnp.full((1, 128), jnp.max(fastest), F32)
        for source in range(2):
            for i in range(circ):
                PS[source, i, SENT - 1 : SENT] = fastest

        for i in range(0, circ, across):
            for j in range(i, i + across):

                @pl.when(c != j)
                def _(j=j):
                    share(j, 0).start()

            for j in range(i, i + across):
                share(j, 1).start()

        R[0] = PS[0, c]

    @pl.when(r == 0)
    def _():
        ga_up.start()
        ga_down.start()


    turn.wait()
    mode = c * MODES_HERE + edge // 2
    total = circ * nt
    angle = ((mode * rotor[0, 0]) & (total - 1)).astype(F32) * (2.0 * math.pi / total)
    imaginary = lax.rem(edge, 2) == 1
    orient = (2 * r - 1).astype(F32)
    turns[0] = jnp.cos(angle)
    turns[1] = jnp.where(imaginary, orient, -orient) * jnp.sin(angle)

    ga_up.wait_recv()
    ga_down.wait_recv()
    for side, a, sign, alone in ((0, 0, -0.5, y == 0), (1, na - 1, 0.5, y == last)):
        ghost = [jnp.where(alone, S[f, a + 1], GA[side, f]) for f in range(FIELDS)]
        w, _ = primitive(ghost)
        for f in range(FIELDS):
            base[f, a] = base[f, a] + SMOOTH * ghost[f]
            conv[f, a] = conv[f, a] + sign * flux(ghost, w, 0, f)
    for copy in (gc_right, gc_left):
        copy.wait_send()
        copy.wait_recv()

    for side, at, row, sign in ((0, 0, 0, -0.5), (1, nt - 8, 7, 0.5)):
        ghost = [GC[side, f] for f in range(FIELDS)]
        w, _ = primitive(ghost)
        for f in range(FIELDS):
            GC[side, f] = SMOOTH * ghost[f]
            CS[side, f] = sign * flux(ghost, w, 1, f)

        def ghosts(a, side=side, at=at, row=row):
            here, rows = pl.ds(a, 1), pl.ds(at, 8)
            for f in range(FIELDS):
                base[f, a, rows] = base[f, a, rows] + jnp.where(edge == row, GC[side, f, here], 0.0)
                conv[f, a, rows] = conv[f, a, rows] + jnp.where(edge == row, CS[side, f, here], 0.0)

        loop(0, na, ghosts)

    ga_up.wait_send()
    ga_down.wait_send()

    @pl.when(r == 0)
    def _():
        drain(RA.at[pl.ds(0, ax)], a_send)

        @pl.when(y == last)
        def _():
            drain(MB, x_send)

        drain(R.at[:, sent], m_recv)

    @pl.when(r == 1)
    def _():
        drain(RA.at[pl.ds(0, ax - 1)], a_send)

        @pl.when(y == last)
        def _():
            drain(MB.at[pl.ds(0, last)], x_send)

        drain(PS.at[0, pl.ds(1, circ - 1), sent], m_send.at[0])
        drain(PS.at[1, :, sent], m_send.at[1])
        drain(R.at[pl.ds(1, circ - 1), sent], m_recv)


def finish_kernel(base, conv, R, turns, out, out_modes, adv, modes, sems):
    circ, na, nt = R.shape[0], base.shape[1], base.shape[2]
    band = modes.shape[-1]
    lane = lax.broadcasted_iota(jnp.int32, (8, 128), 1)
    edge = lax.broadcasted_iota(jnp.int32, (8, 128), 0)

    fastest = R[0, SENT - 1 : SENT]
    for i in range(1, circ):
        fastest = jnp.maximum(fastest, R[i, SENT - 1 : SENT])
    step = 0.8 / (3.0 * jnp.broadcast_to(fastest, (nt, 128)))
    copies = []
    for f in range(FIELDS):
        for a in range(na):
            adv[f, a] = base[f, a] - step * conv[f, a]
        copies.append(pltpu.make_async_copy(adv.at[f], out.at[0, f], sems.at[f]))
        copies[-1].start()

    sums, tail = R[0, 0:8], R[0, 8 : SENT - 1]
    for i in range(1, circ):
        sums, tail = sums + R[i, 0:8], tail + R[i, 8 : SENT - 1]
    tail = jnp.concatenate([tail, jnp.zeros((17 - SENT, 128), F32)], axis=0)
    moved = pltpu.roll(sums, 128 - band * FIELDS, 1)
    for i in range(4):
        piece = pltpu.roll(tail, (band * 3 - 32 * i) % 128, 1)
        piece = pltpu.roll(piece, 2 * i, 0) if i else piece
        moved = jnp.where((edge // 2 == i) & (lane >= band * 3), piece, moved)
    own = sums - step[:8] * moved
    other = jnp.where(lax.rem(edge, 2) == 1, pltpu.roll(own, 1, 0), pltpu.roll(own, 7, 0))
    value = own * turns[0] + other * turns[1]
    for f in range(FIELDS):
        here = pltpu.roll(value, 128 - band * f, 1) if f else value
        for i in range(MODES_HERE):
            for part in range(2):
                row = 2 * i + part
                modes[0, i, f, part : part + 1] = here[row : row + 1, :band]
    copies.append(pltpu.make_async_copy(modes, out_modes, sems.at[FIELDS]))
    copies[-1].start()
    for copy in copies:
        copy.wait()


def on_device(circ, ax, state, rotor_step):
    na, nt = state.shape[2], state.shape[3]
    table = jnp.asarray(tables(circ, nt))
    hbm = pl.BlockSpec(memory_space=pltpu.HBM)
    vmem = pl.BlockSpec(memory_space=pltpu.VMEM)
    dma = pltpu.SemaphoreType.DMA
    block = (FIELDS, na, nt, 128)
    results = pl.pallas_call(
        functools.partial(comm_kernel, circ, 4 if circ % 4 == 0 else 1, ax),
        out_shape=[
            pltpu.VMEM(block, F32),
            pltpu.VMEM(block, F32),
            pltpu.VMEM((circ, 16, 128), F32),
            pltpu.VMEM((2, 8, 128), F32),
        ],
        in_specs=[hbm, hbm, hbm],
        out_specs=[vmem] * 4,
        scratch_shapes=[
            pltpu.VMEM((FIELDS, na + 2, nt, 128), F32),
            pltpu.VMEM((4, na + 2, nt, 128), F32),
            pltpu.VMEM((2, FIELDS, nt, 128), F32),
            pltpu.VMEM((2, FIELDS, na, 128), F32),
            pltpu.VMEM((2, FIELDS, na, 128), F32),
            pltpu.VMEM((circ * 8, DEPTH), F32),
            pltpu.VMEM((4, circ * 8, DEPTH), jnp.bfloat16),
            pltpu.VMEM((ax, BAND_ROWS, 128), F32),
            pltpu.VMEM((2, BAND_ROWS, 128), F32),
            pltpu.VMEM((2, circ, 16, 128), F32),
            pltpu.VMEM((1, 128), F32),
            pltpu.VMEM((2 * ax, 1, 128), F32),
            pltpu.SMEM((1, 1), jnp.int32),
            dma, dma, dma, dma((2,)), dma((2,)), dma((2,)), dma((2,)),
            dma, dma((2,)), dma, dma, dma((2,)), dma,
        ],
        compiler_params=pltpu.CompilerParams(
            collective_id=0, has_side_effects=True, vmem_limit_bytes=56 * 2**20
        ),
        name="exchange",
    )(state, rotor_step.reshape(1, 1), table)
    return pl.pallas_call(
        finish_kernel,
        out_shape=[
            jax.ShapeDtypeStruct(state.shape, F32),
            jax.ShapeDtypeStruct((1, MODES_HERE, FIELDS, 2, 128 // ax), F32),
        ],
        in_specs=[vmem] * 4,
        out_specs=[hbm, hbm],
        scratch_shapes=[
            pltpu.VMEM(block, F32),
            pltpu.VMEM((1, MODES_HERE, FIELDS, 2, 128 // ax), F32),
            dma((FIELDS + 1,)),
        ],
        compiler_params=pltpu.CompilerParams(vmem_limit_bytes=16 * 2**20),
        name="finish",
    )(*(pltpu.with_memory_space_constraint(v, pltpu.VMEM) for v in results))


def solution(mesh):
    return jax.shard_map(
        functools.partial(on_device, mesh.shape["circ"], mesh.shape["ax"]),
        mesh=mesh,
        in_specs=(P("row", None, "ax", "circ", None), P()),
        out_specs=(P("row", None, "ax", "circ", None), P("row", "circ", None, None, "ax")),
        check_vma=False,
    )
```

```python
import functools
import math

import jax
import jax.numpy as jnp
import numpy as np
from jax import lax
from jax.experimental import pallas as pl
from jax.experimental.pallas import tpu as pltpu
from jax.sharding import PartitionSpec as P

MESH = pl.DeviceIdType.MESH
F32 = jnp.float32
FIELDS = 5
MODES_HERE = 4
ROWS = 40
DEPTH = 128
BAND_ROWS = 48
SENT = 11
SMOOTH = 0.8 / 6.0


def tables(circ, cells):
    total = circ * cells
    sector = np.arange(circ)[:, None]
    position = np.zeros((circ, ROWS), np.int64)
    position[:, :cells] = sector * cells + np.arange(cells)[None]
    position[:, cells] = sector[:, 0] * cells + cells
    position[:, cells + 1] = sector[:, 0] * cells - 1
    valid = np.arange(ROWS) < cells + 2
    owner, inner, part = np.meshgrid(np.arange(circ), np.arange(MODES_HERE), np.arange(2), indexing="ij")
    mode = (owner * MODES_HERE + inner).reshape(-1)
    part = part.reshape(-1)
    phase = (mode[None, :, None] * position[:, None, :]) % total
    angle = phase * (2.0 * math.pi / total)
    value = np.where(part[None, :, None] == 0, np.cos(angle), -np.sin(angle)) * math.sqrt(2.0 / total)
    value = np.where(valid[None, None], value, 0.0).astype(np.float32)
    high = value.astype(jnp.bfloat16).astype(np.float32)
    low = (value - high).astype(jnp.bfloat16).astype(np.float32)
    rest = np.zeros((circ, value.shape[1], DEPTH - 3 * ROWS), np.float32)
    return np.concatenate([high, high, low, rest], axis=2)


def flux(q, w, d, f):
    value = q[f] * w[d]
    if f == 1 + d:
        value = value + w[3]
    if f == 4:
        value = value + w[3] * w[d]
    return value


def primitive(q):
    inverse = 1.0 / q[0]
    u = [q[1 + d] * inverse for d in range(3)]
    p = 0.4 * (q[4] - 0.5 * (q[1] * u[0] + q[2] * u[1] + q[3] * u[2]))
    return u + [p], inverse


def lanes_next(v, lane):
    return jnp.where(lane == 127, v, pltpu.roll(v, 127, 1))


def lanes_prev(v, lane):
    return jnp.where(lane == 0, v, pltpu.roll(v, 1, 1))


def distance(n, d):
    return min(d, n - d)


def offsets(first, second):
    pairs = [(d, e) for d in range(first) for e in range(second)]
    return sorted(pairs, key=lambda p: (-distance(first, p[0]) - distance(second, p[1]), p == (0, 0)))


def comm_kernel(
    circ, across, ax,
    st, rot, tab, base, conv, R, turns,
    S, W, GA, GC, CS, E, EB, MB, XR, PS, MA, RA,
    rotor, load_sem, tab_sem, rot_sem, ga_send, ga_recv, gc_send, gc_recv,
    x_send, x_recv, a_send, a_recv, m_send, m_recv,
):
    r, c, y = lax.axis_index("row"), lax.axis_index("circ"), lax.axis_index("ax")
    na, nt = S.shape[1] - 2, S.shape[2]
    last = ax - 1
    load = pltpu.make_async_copy(st.at[0], S.at[:, pl.ds(1, na)], load_sem)
    load.start()
    table = pltpu.make_async_copy(tab.at[c], E, tab_sem)
    table.start()
    turn = pltpu.make_async_copy(rot, rotor, rot_sem)
    turn.start()

    lines = [lax.rem(y + d, ax) for d in range(ax)]
    near_offsets, far_offsets = offsets(ax, 2), offsets(circ // across, across)[:-1]
    layers = [lax.rem(c // across + d, circ // across) * across for d in range(circ // across)]
    columns = [lax.rem(lax.rem(c, across) + d, across) for d in range(across)]
    right, left = (r, lax.rem(c + 1, circ), y), (r, lax.rem(c + circ - 1, circ), y)
    up, down = (r, c, lines[1]), (r, c, lines[last])
    barrier = pltpu.get_barrier_semaphore()

    def greet(device):
        pl.semaphore_signal(barrier, inc=1, device_id=device, device_id_type=MESH)

    def loop(lo, hi, body):
        def step(i, carry):
            body(i)
            return carry

        lax.fori_loop(lo, hi, step, 0)

    @pl.when(r == 0)
    def _():
        for device in (up, down, left, right):
            greet(device)
        greet((1, c, y))

    @pl.when(r == 1)
    def _():
        for d, e in near_offsets[:-1]:
            greet((1 - e, c, lines[d]))

    for d, e in far_offsets:
        greet((1, layers[d] + columns[e], y))

    load.wait()

    def speeds(a, fastest):
        q = [S[f, a] for f in range(FIELDS)]
        w, inverse = primitive(q)
        for i in range(4):
            W[i, a] = w[i]
        speed = jnp.maximum(jnp.maximum(jnp.abs(w[0]), jnp.abs(w[1])), jnp.abs(w[2]))
        speed = speed + jnp.sqrt(1.4 * w[3] * inverse)
        for i in range(nt // 8):
            fastest = jnp.maximum(fastest, speed[8 * i : 8 * i + 8])
        return fastest

    MA[...] = jnp.max(lax.fori_loop(1, na + 1, speeds, jnp.zeros((8, 128), F32)), axis=0, keepdims=True)
    @pl.when(r == 0)
    def _():
        pl.semaphore_wait(barrier, ax + 4)

    @pl.when(r == 1)
    def _():
        pl.semaphore_wait(barrier, ax - 1 + 2 * circ - 1)

    def send(src, dst, sent, got, device):
        return pltpu.make_async_remote_copy(
            src_ref=src, dst_ref=dst, send_sem=sent, recv_sem=got, device_id=device, device_id_type=MESH
        )

    def drain(ref, sem):
        pltpu.make_async_copy(ref, ref, sem).wait()

    def band_to(k):
        return send(MB.at[k], XR.at[r], x_send, x_recv.at[r], (1, c, k))

    by_distance = sorted(range(ax), key=lambda k: (k == last, distance(ax, k)))

    def speed_to(i):
        send(MA, RA.at[i], a_send, a_recv, (1, c, lines[near_offsets[i][0]])).start()

    @pl.when(r == 0)
    def _():
        for i in range(2 * ax - 1):
            if near_offsets[i][1]:
                speed_to(i)

    @pl.when(r == 1)
    def _():
        for i in range(2 * ax - 1):
            if not near_offsets[i][1]:
                speed_to(i)

    for f in range(FIELDS):
        CS[0, f] = S[f, 1 : na + 1, nt - 1]
        CS[1, f] = S[f, 1 : na + 1, 0]

    lane = lax.broadcasted_iota(jnp.int32, (nt, 128), 1)
    cell = lax.broadcasted_iota(jnp.int32, (nt, 128), 0)
    edge = lax.broadcasted_iota(jnp.int32, (8, 128), 0)

    def inside_next(v):
        return jnp.where(cell == nt - 1, 0.0, pltpu.roll(v, nt - 1, 0))

    def inside_prev(v):
        return jnp.where(cell == 0, 0.0, pltpu.roll(v, 1, 0))

    def plane(a):
        q, w = [S[f, a] for f in range(FIELDS)], [W[i, a] for i in range(4)]
        qu, wu = [S[f, a + 1] for f in range(FIELDS)], [W[i, a + 1] for i in range(4)]
        qd, wd = [S[f, a - 1] for f in range(FIELDS)], [W[i, a - 1] for i in range(4)]
        for f in range(FIELDS):
            qf = q[f]
            smooth = qu[f] + qd[f] - 6.0 * qf + lanes_next(qf, lane) + lanes_prev(qf, lane)
            base[f, a - 1] = qf + SMOOTH * (smooth + inside_next(qf) + inside_prev(qf))
            f1, f2 = flux(q, w, 1, f), flux(q, w, 2, f)
            moved = flux(qu, wu, 0, f) - flux(qd, wd, 0, f)
            moved = moved + lanes_next(f2, lane) - lanes_prev(f2, lane)
            conv[f, a - 1] = 0.5 * (moved + inside_next(f1) - inside_prev(f1))

    for a in (0, na + 1):
        for f in range(FIELDS):
            S[f, a] = jnp.zeros((nt, 128), F32)
        for i in range(4):
            W[i, a] = jnp.zeros((nt, 128), F32)

    band = 128 // ax

    @pl.when(y == last)
    def _():
        q = [S[f, na] for f in range(FIELDS)]
        w = [W[i, na] for i in range(4)]
        qm = [S[f, na - 1] for f in range(FIELDS)]
        wm = [W[i, na - 1] for i in range(4)]
        group = lax.broadcasted_iota(jnp.int32, (ROWS, 128), 1) // band
        quarter = group[:8] // 2
        terms = [[], []]

        for f in range(FIELDS):
            qf = q[f]
            smooth = qm[f] - 5.0 * qf + lanes_next(qf, lane) + lanes_prev(qf, lane)
            smooth = smooth + inside_next(qf) + inside_prev(qf)
            still = qf + SMOOTH * smooth
            f1, f2 = flux(q, w, 1, f), flux(q, w, 2, f)
            moved = flux(q, w, 0, f) - flux(qm, wm, 0, f)
            moved = moved + lanes_next(f2, lane) - lanes_prev(f2, lane)
            moved = 0.5 * (moved + inside_next(f1) - inside_prev(f1))
            q_ends = jnp.where(edge == 0, qf[nt - 1 : nt], jnp.where(edge == 1, qf[0:1], 0.0))
            f_ends = jnp.where(edge == 0, -f1[nt - 1 : nt], jnp.where(edge == 1, f1[0:1], 0.0))
            for part, (inner, ends) in enumerate(((still, SMOOTH * q_ends), (moved, 0.5 * f_ends))):
                whole = jnp.concatenate([inner, ends], axis=0)
                terms[part].append(whole)
        terms = terms[0] + terms[1]
        placed = [pltpu.roll(v, band * g, 1) if g else v for g, v in enumerate(terms[:8])]
        others = [terms[8], pltpu.roll(terms[9], band, 1)]
        for k in range(ax):
            chosen = placed[0]
            for g in range(1, 8):
                chosen = jnp.where(group == (g + k) % ax, placed[g], chosen)
            chosen = pltpu.roll(chosen, 128 - band * k, 1) if k else chosen
            rest = jnp.where(group == k, others[0], others[1])
            turned = [pltpu.roll(rest[8 * i : 8 * i + 8], (32 * i - band * k) % 128, 1) for i in range(5)]
            MB[k, : ROWS - 8] = chosen[: ROWS - 8]
            MB[k, ROWS - 8 : ROWS] = jnp.where(edge < 2, chosen[ROWS - 8 :], pltpu.roll(turned[4], 2, 0))
            for i in range(1, 4):
                turned[0] = jnp.where(quarter == i, turned[i], turned[0])
            MB[k, ROWS:] = turned[0]
        XR[1] = MB[last]

    @pl.when(y == last)
    def _():
        for k in by_distance[:-1]:
            band_to(k).start()

        @pl.when(r == 0)
        def _():
            band_to(last).start()

    gc_right = send(CS.at[0], GC.at[0], gc_send.at[0], gc_recv.at[0], right)
    gc_left = send(CS.at[1], GC.at[1], gc_send.at[1], gc_recv.at[1], left)
    gc_right.start()
    gc_left.start()
    ga_up = send(S.at[:, na], GA.at[0], ga_send.at[0], ga_recv.at[0], up)
    ga_down = send(S.at[:, 1], GA.at[1], ga_send.at[1], ga_recv.at[1], down)

    @pl.when(r == 0)
    def _():
        ga_up.start()
        ga_down.start()

    loop(1, na + 1, plane)
    table.wait()

    @pl.when(r == 1)
    def _():
        factors = E[...].reshape(circ, 8, DEPTH)
        for i in range(4):
            rows = pltpu.roll(factors, 8 - 2 * i, 1) if i else factors
            EB[i] = rows.reshape(circ * 8, DEPTH).astype(jnp.bfloat16)

    sent = pl.ds(0, SENT)

    def split(v):
        high = v.astype(jnp.bfloat16).astype(F32)
        parts = [high, v - high, high, jnp.zeros((DEPTH - 3 * ROWS, 128), F32)]
        return jnp.concatenate(parts, axis=0).astype(jnp.bfloat16)

    def share(i, source):
        device, slot = (1 - source, i, y), lax.rem(c - i + circ, circ)
        return send(PS.at[source, i, sent], R.at[slot, sent], m_send.at[source], m_recv, device)

    @pl.when(r == 1)
    def _():
        drain(XR.at[0], x_recv.at[0])

        @pl.when(y != last)
        def _():
            drain(XR.at[1], x_recv.at[1])

        ga_up.start()
        ga_down.start()
        eight, others = [], []
        for source in range(2):
            packed = XR[source, ROWS:]
            rest = [pltpu.roll(packed, 128 - 32 * i, 1) if i else packed for i in range(4)]
            rest = jnp.concatenate(rest + [pltpu.roll(XR[source, ROWS - 8 : ROWS], 6, 0)], axis=0)
            rest = jnp.where(lax.broadcasted_iota(jnp.int32, (ROWS, 128), 1) < 32, rest, 0.0)
            eight.append(split(XR[source, :ROWS]))
            others.append([split(pltpu.roll(rest, 32 * i, 1) if i else rest) for i in range(4)])

        def dot(i, v):
            return jnp.dot(EB[i], v, preferred_element_type=F32).reshape(circ, 8, v.shape[1])

        first = dot(0, jnp.concatenate(eight, axis=1))
        second = dot(0, jnp.concatenate([others[0][0], others[1][0]], axis=1))
        for i in range(1, 4):
            second = second + dot(i, jnp.concatenate([others[0][i], others[1][i]], axis=1))
        for source in range(2):
            lanes = slice(128 * source, 128 * source + 128)
            PS[source, :, 0:8] = first[:, :, lanes]
            PS[source, :, 8:16] = second[:, :, lanes]
        drain(RA.at[pl.ds(0, 2 * ax - 1)], a_recv)
        fastest = MA[...]
        for i in range(2 * ax - 1):
            fastest = jnp.maximum(fastest, RA[i])
        fastest = jnp.full((1, 128), jnp.max(fastest), F32)
        for source in range(2):
            for i in range(circ):
                PS[source, i, SENT - 1 : SENT] = fastest

        for i in range(0, circ, across):
            for j in range(i, i + across):

                @pl.when(c != j)
                def _(j=j):
                    share(j, 0).start()

            for j in range(i, i + across):
                share(j, 1).start()

        R[0] = PS[0, c]


    turn.wait()
    mode = c * MODES_HERE + edge // 2
    total = circ * nt
    angle = ((mode * rotor[0, 0]) & (total - 1)).astype(F32) * (2.0 * math.pi / total)
    imaginary = lax.rem(edge, 2) == 1
    orient = (2 * r - 1).astype(F32)
    turns[0] = jnp.cos(angle)
    turns[1] = jnp.where(imaginary, orient, -orient) * jnp.sin(angle)

    ga_up.wait_recv()
    ga_down.wait_recv()
    for side, a, sign, alone in ((0, 0, -0.5, y == 0), (1, na - 1, 0.5, y == last)):
        ghost = [jnp.where(alone, S[f, a + 1], GA[side, f]) for f in range(FIELDS)]
        w, _ = primitive(ghost)
        for f in range(FIELDS):
            base[f, a] = base[f, a] + SMOOTH * ghost[f]
            conv[f, a] = conv[f, a] + sign * flux(ghost, w, 0, f)
    for copy in (gc_right, gc_left):
        copy.wait_send()
        copy.wait_recv()

    for side, at, row, sign in ((0, 0, 0, -0.5), (1, nt - 8, 7, 0.5)):
        ghost = [GC[side, f] for f in range(FIELDS)]
        w, _ = primitive(ghost)
        for f in range(FIELDS):
            GC[side, f] = SMOOTH * ghost[f]
            CS[side, f] = sign * flux(ghost, w, 1, f)

        def ghosts(a, side=side, at=at, row=row):
            here, rows = pl.ds(a, 1), pl.ds(at, 8)
            for f in range(FIELDS):
                base[f, a, rows] = base[f, a, rows] + jnp.where(edge == row, GC[side, f, here], 0.0)
                conv[f, a, rows] = conv[f, a, rows] + jnp.where(edge == row, CS[side, f, here], 0.0)

        loop(0, na, ghosts)

    ga_up.wait_send()
    ga_down.wait_send()

    @pl.when(r == 0)
    def _():
        drain(RA.at[pl.ds(0, ax)], a_send)

        @pl.when(y == last)
        def _():
            drain(MB, x_send)

        drain(R.at[:, sent], m_recv)

    @pl.when(r == 1)
    def _():
        drain(RA.at[pl.ds(0, ax - 1)], a_send)

        @pl.when(y == last)
        def _():
            drain(MB.at[pl.ds(0, last)], x_send)

        drain(PS.at[0, pl.ds(1, circ - 1), sent], m_send.at[0])
        drain(PS.at[1, :, sent], m_send.at[1])
        drain(R.at[pl.ds(1, circ - 1), sent], m_recv)


def finish_kernel(base, conv, R, turns, out, out_modes, adv, modes, sems):
    circ, na, nt = R.shape[0], base.shape[1], base.shape[2]
    band = modes.shape[-1]
    lane = lax.broadcasted_iota(jnp.int32, (8, 128), 1)
    edge = lax.broadcasted_iota(jnp.int32, (8, 128), 0)

    fastest = R[0, SENT - 1 : SENT]
    for i in range(1, circ):
        fastest = jnp.maximum(fastest, R[i, SENT - 1 : SENT])
    step = 0.8 / (3.0 * jnp.broadcast_to(fastest, (nt, 128)))
    copies = []
    for f in range(FIELDS):
        for a in range(na):
            adv[f, a] = base[f, a] - step * conv[f, a]
        copies.append(pltpu.make_async_copy(adv.at[f], out.at[0, f], sems.at[f]))
        copies[-1].start()

    sums, tail = R[0, 0:8], R[0, 8 : SENT - 1]
    for i in range(1, circ):
        sums, tail = sums + R[i, 0:8], tail + R[i, 8 : SENT - 1]
    tail = jnp.concatenate([tail, jnp.zeros((17 - SENT, 128), F32)], axis=0)
    moved = pltpu.roll(sums, 128 - band * FIELDS, 1)
    for i in range(4):
        piece = pltpu.roll(tail, (band * 3 - 32 * i) % 128, 1)
        piece = pltpu.roll(piece, 2 * i, 0) if i else piece
        moved = jnp.where((edge // 2 == i) & (lane >= band * 3), piece, moved)
    own = sums - step[:8] * moved
    other = jnp.where(lax.rem(edge, 2) == 1, pltpu.roll(own, 1, 0), pltpu.roll(own, 7, 0))
    value = own * turns[0] + other * turns[1]
    for f in range(FIELDS):
        here = pltpu.roll(value, 128 - band * f, 1) if f else value
        for i in range(MODES_HERE):
            for part in range(2):
                row = 2 * i + part
                modes[0, i, f, part : part + 1] = here[row : row + 1, :band]
    copies.append(pltpu.make_async_copy(modes, out_modes, sems.at[FIELDS]))
    copies[-1].start()
    for copy in copies:
        copy.wait()


def on_device(circ, ax, state, rotor_step):
    na, nt = state.shape[2], state.shape[3]
    table = jnp.asarray(tables(circ, nt))
    hbm = pl.BlockSpec(memory_space=pltpu.HBM)
    vmem = pl.BlockSpec(memory_space=pltpu.VMEM)
    dma = pltpu.SemaphoreType.DMA
    block = (FIELDS, na, nt, 128)
    results = pl.pallas_call(
        functools.partial(comm_kernel, circ, 4 if circ % 4 == 0 else 1, ax),
        out_shape=[
            pltpu.VMEM(block, F32),
            pltpu.VMEM(block, F32),
            pltpu.VMEM((circ, 16, 128), F32),
            pltpu.VMEM((2, 8, 128), F32),
        ],
        in_specs=[hbm, hbm, hbm],
        out_specs=[vmem] * 4,
        scratch_shapes=[
            pltpu.VMEM((FIELDS, na + 2, nt, 128), F32),
            pltpu.VMEM((4, na + 2, nt, 128), F32),
            pltpu.VMEM((2, FIELDS, nt, 128), F32),
            pltpu.VMEM((2, FIELDS, na, 128), F32),
            pltpu.VMEM((2, FIELDS, na, 128), F32),
            pltpu.VMEM((circ * 8, DEPTH), F32),
            pltpu.VMEM((4, circ * 8, DEPTH), jnp.bfloat16),
            pltpu.VMEM((ax, BAND_ROWS, 128), F32),
            pltpu.VMEM((2, BAND_ROWS, 128), F32),
            pltpu.VMEM((2, circ, 16, 128), F32),
            pltpu.VMEM((1, 128), F32),
            pltpu.VMEM((2 * ax, 1, 128), F32),
            pltpu.SMEM((1, 1), jnp.int32),
            dma, dma, dma, dma((2,)), dma((2,)), dma((2,)), dma((2,)),
            dma, dma((2,)), dma, dma, dma((2,)), dma,
        ],
        compiler_params=pltpu.CompilerParams(
            collective_id=0, has_side_effects=True, vmem_limit_bytes=56 * 2**20
        ),
        name="exchange",
    )(state, rotor_step.reshape(1, 1), table)
    return pl.pallas_call(
        finish_kernel,
        out_shape=[
            jax.ShapeDtypeStruct(state.shape, F32),
            jax.ShapeDtypeStruct((1, MODES_HERE, FIELDS, 2, 128 // ax), F32),
        ],
        in_specs=[vmem] * 4,
        out_specs=[hbm, hbm],
        scratch_shapes=[
            pltpu.VMEM(block, F32),
            pltpu.VMEM((1, MODES_HERE, FIELDS, 2, 128 // ax), F32),
            dma((FIELDS + 1,)),
        ],
        compiler_params=pltpu.CompilerParams(vmem_limit_bytes=16 * 2**20),
        name="finish",
    )(*(pltpu.with_memory_space_constraint(v, pltpu.VMEM) for v in results))


def solution(mesh):
    return jax.shard_map(
        functools.partial(on_device, mesh.shape["circ"], mesh.shape["ax"]),
        mesh=mesh,
        in_specs=(P("row", None, "ax", "circ", None), P()),
        out_specs=(P("row", None, "ax", "circ", None), P("row", "circ", None, None, "ax")),
        check_vma=False,
    )
```

```python
import functools
import math

import jax
import jax.numpy as jnp
import numpy as np
from jax import lax
from jax.experimental import pallas as pl
from jax.experimental.pallas import tpu as pltpu
from jax.sharding import PartitionSpec as P

MESH = pl.DeviceIdType.MESH
F32 = jnp.float32
FIELDS = 5
MODES_HERE = 4
ROWS = 40
DEPTH = 128
BAND_ROWS = 48
SENT = 11
SMOOTH = 0.8 / 6.0


def tables(circ, cells):
    total = circ * cells
    sector = np.arange(circ)[:, None]
    position = np.zeros((circ, ROWS), np.int64)
    position[:, :cells] = sector * cells + np.arange(cells)[None]
    position[:, cells] = sector[:, 0] * cells + cells
    position[:, cells + 1] = sector[:, 0] * cells - 1
    valid = np.arange(ROWS) < cells + 2
    owner, inner, part = np.meshgrid(np.arange(circ), np.arange(MODES_HERE), np.arange(2), indexing="ij")
    mode = (owner * MODES_HERE + inner).reshape(-1)
    part = part.reshape(-1)
    phase = (mode[None, :, None] * position[:, None, :]) % total
    angle = phase * (2.0 * math.pi / total)
    value = np.where(part[None, :, None] == 0, np.cos(angle), -np.sin(angle)) * math.sqrt(2.0 / total)
    value = np.where(valid[None, None], value, 0.0).astype(np.float32)
    high = value.astype(jnp.bfloat16).astype(np.float32)
    low = (value - high).astype(jnp.bfloat16).astype(np.float32)
    rest = np.zeros((circ, value.shape[1], DEPTH - 3 * ROWS), np.float32)
    return np.concatenate([high, high, low, rest], axis=2)


def flux(q, w, d, f):
    value = q[f] * w[d]
    if f == 1 + d:
        value = value + w[3]
    if f == 4:
        value = value + w[3] * w[d]
    return value


def primitive(q):
    inverse = 1.0 / q[0]
    u = [q[1 + d] * inverse for d in range(3)]
    p = 0.4 * (q[4] - 0.5 * (q[1] * u[0] + q[2] * u[1] + q[3] * u[2]))
    return u + [p], inverse


def lanes_next(v, lane):
    return jnp.where(lane == 127, v, pltpu.roll(v, 127, 1))


def lanes_prev(v, lane):
    return jnp.where(lane == 0, v, pltpu.roll(v, 1, 1))


def distance(n, d):
    return min(d, n - d)


def offsets(first, second):
    pairs = [(d, e) for d in range(first) for e in range(second)]
    return sorted(pairs, key=lambda p: (-distance(first, p[0]) - distance(second, p[1]), p == (0, 0)))


def comm_kernel(
    circ, across, ax,
    st, rot, tab, base, conv, R, turns,
    S, W, GA, GC, CS, E, EB, MB, XR, PS, MA, RA,
    rotor, load_sem, tab_sem, rot_sem, ga_send, ga_recv, gc_send, gc_recv,
    x_send, x_recv, a_send, a_recv, m_send, m_recv,
):
    r, c, y = lax.axis_index("row"), lax.axis_index("circ"), lax.axis_index("ax")
    na, nt = S.shape[1] - 2, S.shape[2]
    last = ax - 1
    load = pltpu.make_async_copy(st.at[0], S.at[:, pl.ds(1, na)], load_sem)
    load.start()
    table = pltpu.make_async_copy(tab.at[c], E, tab_sem)
    table.start()
    turn = pltpu.make_async_copy(rot, rotor, rot_sem)
    turn.start()

    lines = [lax.rem(y + d, ax) for d in range(ax)]
    near_offsets, far_offsets = offsets(ax, 2), offsets(circ // across, across)[:-1]
    layers = [lax.rem(c // across + d, circ // across) * across for d in range(circ // across)]
    columns = [lax.rem(lax.rem(c, across) + d, across) for d in range(across)]
    right, left = (r, lax.rem(c + 1, circ), y), (r, lax.rem(c + circ - 1, circ), y)
    up, down = (r, c, lines[1]), (r, c, lines[last])
    barrier = pltpu.get_barrier_semaphore()

    def greet(device):
        pl.semaphore_signal(barrier, inc=1, device_id=device, device_id_type=MESH)

    def loop(lo, hi, body):
        def step(i, carry):
            body(i)
            return carry

        lax.fori_loop(lo, hi, step, 0)

    @pl.when(r == 0)
    def _():
        for device in (up, down, left, right):
            greet(device)
        greet((1, c, y))

    @pl.when(r == 1)
    def _():
        for d, e in near_offsets[:-1]:
            greet((1 - e, c, lines[d]))

    for d, e in far_offsets:
        greet((1, layers[d] + columns[e], y))

    load.wait()

    def speeds(a, fastest):
        q = [S[f, a] for f in range(FIELDS)]
        w, inverse = primitive(q)
        for i in range(4):
            W[i, a] = w[i]
        speed = jnp.maximum(jnp.maximum(jnp.abs(w[0]), jnp.abs(w[1])), jnp.abs(w[2]))
        speed = speed + jnp.sqrt(1.4 * w[3] * inverse)
        for i in range(nt // 8):
            fastest = jnp.maximum(fastest, speed[8 * i : 8 * i + 8])
        return fastest

    MA[...] = jnp.max(lax.fori_loop(1, na + 1, speeds, jnp.zeros((8, 128), F32)), axis=0, keepdims=True)
    for f in range(FIELDS):
        CS[0, f] = S[f, 1 : na + 1, nt - 1]
        CS[1, f] = S[f, 1 : na + 1, 0]

    lane = lax.broadcasted_iota(jnp.int32, (nt, 128), 1)
    cell = lax.broadcasted_iota(jnp.int32, (nt, 128), 0)
    edge = lax.broadcasted_iota(jnp.int32, (8, 128), 0)

    def inside_next(v):
        return jnp.where(cell == nt - 1, 0.0, pltpu.roll(v, nt - 1, 0))

    def inside_prev(v):
        return jnp.where(cell == 0, 0.0, pltpu.roll(v, 1, 0))

    def plane(a):
        q, w = [S[f, a] for f in range(FIELDS)], [W[i, a] for i in range(4)]
        qu, wu = [S[f, a + 1] for f in range(FIELDS)], [W[i, a + 1] for i in range(4)]
        qd, wd = [S[f, a - 1] for f in range(FIELDS)], [W[i, a - 1] for i in range(4)]
        for f in range(FIELDS):
            qf = q[f]
            smooth = qu[f] + qd[f] - 6.0 * qf + lanes_next(qf, lane) + lanes_prev(qf, lane)
            base[f, a - 1] = qf + SMOOTH * (smooth + inside_next(qf) + inside_prev(qf))
            f1, f2 = flux(q, w, 1, f), flux(q, w, 2, f)
            moved = flux(qu, wu, 0, f) - flux(qd, wd, 0, f)
            moved = moved + lanes_next(f2, lane) - lanes_prev(f2, lane)
            conv[f, a - 1] = 0.5 * (moved + inside_next(f1) - inside_prev(f1))

    for a in (0, na + 1):
        for f in range(FIELDS):
            S[f, a] = jnp.zeros((nt, 128), F32)
        for i in range(4):
            W[i, a] = jnp.zeros((nt, 128), F32)

    band = 128 // ax

    @pl.when(y == last)
    def _():
        q = [S[f, na] for f in range(FIELDS)]
        w = [W[i, na] for i in range(4)]
        qm = [S[f, na - 1] for f in range(FIELDS)]
        wm = [W[i, na - 1] for i in range(4)]
        group = lax.broadcasted_iota(jnp.int32, (ROWS, 128), 1) // band
        quarter = group[:8] // 2
        terms = [[], []]

        for f in range(FIELDS):
            qf = q[f]
            smooth = qm[f] - 5.0 * qf + lanes_next(qf, lane) + lanes_prev(qf, lane)
            smooth = smooth + inside_next(qf) + inside_prev(qf)
            still = qf + SMOOTH * smooth
            f1, f2 = flux(q, w, 1, f), flux(q, w, 2, f)
            moved = flux(q, w, 0, f) - flux(qm, wm, 0, f)
            moved = moved + lanes_next(f2, lane) - lanes_prev(f2, lane)
            moved = 0.5 * (moved + inside_next(f1) - inside_prev(f1))
            q_ends = jnp.where(edge == 0, qf[nt - 1 : nt], jnp.where(edge == 1, qf[0:1], 0.0))
            f_ends = jnp.where(edge == 0, -f1[nt - 1 : nt], jnp.where(edge == 1, f1[0:1], 0.0))
            for part, (inner, ends) in enumerate(((still, SMOOTH * q_ends), (moved, 0.5 * f_ends))):
                whole = jnp.concatenate([inner, ends], axis=0)
                terms[part].append(whole)
        terms = terms[0] + terms[1]
        placed = [pltpu.roll(v, band * g, 1) if g else v for g, v in enumerate(terms[:8])]
        others = [terms[8], pltpu.roll(terms[9], band, 1)]
        for k in range(ax):
            chosen = placed[0]
            for g in range(1, 8):
                chosen = jnp.where(group == (g + k) % ax, placed[g], chosen)
            chosen = pltpu.roll(chosen, 128 - band * k, 1) if k else chosen
            rest = jnp.where(group == k, others[0], others[1])
            turned = [pltpu.roll(rest[8 * i : 8 * i + 8], (32 * i - band * k) % 128, 1) for i in range(5)]
            MB[k, : ROWS - 8] = chosen[: ROWS - 8]
            MB[k, ROWS - 8 : ROWS] = jnp.where(edge < 2, chosen[ROWS - 8 :], pltpu.roll(turned[4], 2, 0))
            for i in range(1, 4):
                turned[0] = jnp.where(quarter == i, turned[i], turned[0])
            MB[k, ROWS:] = turned[0]
        XR[1] = MB[last]

    @pl.when(r == 0)
    def _():
        pl.semaphore_wait(barrier, ax + 4)

    @pl.when(r == 1)
    def _():
        pl.semaphore_wait(barrier, ax - 1 + 2 * circ - 1)

    def send(src, dst, sent, got, device):
        return pltpu.make_async_remote_copy(
            src_ref=src, dst_ref=dst, send_sem=sent, recv_sem=got, device_id=device, device_id_type=MESH
        )

    def drain(ref, sem):
        pltpu.make_async_copy(ref, ref, sem).wait()

    def band_to(k):
        return send(MB.at[k], XR.at[r], x_send, x_recv.at[r], (1, c, k))

    by_distance = sorted(range(ax), key=lambda k: (k == last, distance(ax, k)))

    def speed_to(i):
        send(MA, RA.at[i], a_send, a_recv, (1, c, lines[near_offsets[i][0]])).start()

    @pl.when(r == 0)
    def _():
        for i in range(2 * ax - 1):
            if near_offsets[i][1]:
                speed_to(i)

    @pl.when(r == 1)
    def _():
        for i in range(2 * ax - 1):
            if not near_offsets[i][1]:
                speed_to(i)

    @pl.when(y == last)
    def _():
        for k in by_distance[:-1]:
            band_to(k).start()

        @pl.when(r == 0)
        def _():
            band_to(last).start()

    gc_right = send(CS.at[0], GC.at[0], gc_send.at[0], gc_recv.at[0], right)
    gc_left = send(CS.at[1], GC.at[1], gc_send.at[1], gc_recv.at[1], left)
    gc_right.start()
    gc_left.start()
    ga_up = send(S.at[:, na], GA.at[0], ga_send.at[0], ga_recv.at[0], up)
    ga_down = send(S.at[:, 1], GA.at[1], ga_send.at[1], ga_recv.at[1], down)

    loop(1, na + 1, plane)
    table.wait()

    @pl.when(r == 1)
    def _():
        factors = E[...].reshape(circ, 8, DEPTH)
        for i in range(4):
            rows = pltpu.roll(factors, 8 - 2 * i, 1) if i else factors
            EB[i] = rows.reshape(circ * 8, DEPTH).astype(jnp.bfloat16)

    sent = pl.ds(0, SENT)

    def split(v):
        high = v.astype(jnp.bfloat16).astype(F32)
        parts = [high, v - high, high, jnp.zeros((DEPTH - 3 * ROWS, 128), F32)]
        return jnp.concatenate(parts, axis=0).astype(jnp.bfloat16)

    def share(i, source):
        device, slot = (1 - source, i, y), lax.rem(c - i + circ, circ)
        return send(PS.at[source, i, sent], R.at[slot, sent], m_send.at[source], m_recv, device)

    @pl.when(r == 1)
    def _():
        drain(XR.at[0], x_recv.at[0])

        @pl.when(y != last)
        def _():
            drain(XR.at[1], x_recv.at[1])

        ga_up.start()
        ga_down.start()
        eight, others = [], []
        for source in range(2):
            packed = XR[source, ROWS:]
            rest = [pltpu.roll(packed, 128 - 32 * i, 1) if i else packed for i in range(4)]
            rest = jnp.concatenate(rest + [pltpu.roll(XR[source, ROWS - 8 : ROWS], 6, 0)], axis=0)
            rest = jnp.where(lax.broadcasted_iota(jnp.int32, (ROWS, 128), 1) < 32, rest, 0.0)
            eight.append(split(XR[source, :ROWS]))
            others.append([split(pltpu.roll(rest, 32 * i, 1) if i else rest) for i in range(4)])

        def dot(i, v):
            return jnp.dot(EB[i], v, preferred_element_type=F32).reshape(circ, 8, v.shape[1])

        first = dot(0, jnp.concatenate(eight, axis=1))
        second = dot(0, jnp.concatenate([others[0][0], others[1][0]], axis=1))
        for i in range(1, 4):
            second = second + dot(i, jnp.concatenate([others[0][i], others[1][i]], axis=1))
        for source in range(2):
            lanes = slice(128 * source, 128 * source + 128)
            PS[source, :, 0:8] = first[:, :, lanes]
            PS[source, :, 8:16] = second[:, :, lanes]
        drain(RA.at[pl.ds(0, 2 * ax - 1)], a_recv)
        fastest = MA[...]
        for i in range(2 * ax - 1):
            fastest = jnp.maximum(fastest, RA[i])
        fastest = jnp.full((1, 128), jnp.max(fastest), F32)
        for source in range(2):
            for i in range(circ):
                PS[source, i, SENT - 1 : SENT] = fastest

        for i in range(0, circ, across):
            for j in range(i, i + across):

                @pl.when(c != j)
                def _(j=j):
                    share(j, 0).start()

            for j in range(i, i + across):
                share(j, 1).start()

        R[0] = PS[0, c]

    @pl.when(r == 0)
    def _():
        ga_up.start()
        ga_down.start()


    turn.wait()
    mode = c * MODES_HERE + edge // 2
    total = circ * nt
    angle = ((mode * rotor[0, 0]) & (total - 1)).astype(F32) * (2.0 * math.pi / total)
    imaginary = lax.rem(edge, 2) == 1
    orient = (2 * r - 1).astype(F32)
    turns[0] = jnp.cos(angle)
    turns[1] = jnp.where(imaginary, orient, -orient) * jnp.sin(angle)

    ga_up.wait_recv()
    ga_down.wait_recv()
    for side, a, sign, alone in ((0, 0, -0.5, y == 0), (1, na - 1, 0.5, y == last)):
        ghost = [jnp.where(alone, S[f, a + 1], GA[side, f]) for f in range(FIELDS)]
        w, _ = primitive(ghost)
        for f in range(FIELDS):
            base[f, a] = base[f, a] + SMOOTH * ghost[f]
            conv[f, a] = conv[f, a] + sign * flux(ghost, w, 0, f)
    for copy in (gc_right, gc_left):
        copy.wait_send()
        copy.wait_recv()

    for side, at, row, sign in ((0, 0, 0, -0.5), (1, nt - 8, 7, 0.5)):
        ghost = [GC[side, f] for f in range(FIELDS)]
        w, _ = primitive(ghost)
        for f in range(FIELDS):
            GC[side, f] = SMOOTH * ghost[f]
            CS[side, f] = sign * flux(ghost, w, 1, f)

        def ghosts(a, side=side, at=at, row=row):
            here, rows = pl.ds(a, 1), pl.ds(at, 8)
            for f in range(FIELDS):
                base[f, a, rows] = base[f, a, rows] + jnp.where(edge == row, GC[side, f, here], 0.0)
                conv[f, a, rows] = conv[f, a, rows] + jnp.where(edge == row, CS[side, f, here], 0.0)

        loop(0, na, ghosts)

    ga_up.wait_send()
    ga_down.wait_send()

    @pl.when(r == 0)
    def _():
        drain(RA.at[pl.ds(0, ax)], a_send)

        @pl.when(y == last)
        def _():
            drain(MB, x_send)

        drain(R.at[:, sent], m_recv)

    @pl.when(r == 1)
    def _():
        drain(RA.at[pl.ds(0, ax - 1)], a_send)

        @pl.when(y == last)
        def _():
            drain(MB.at[pl.ds(0, last)], x_send)

        drain(PS.at[0, pl.ds(1, circ - 1), sent], m_send.at[0])
        drain(PS.at[1, :, sent], m_send.at[1])
        drain(R.at[pl.ds(1, circ - 1), sent], m_recv)


def finish_kernel(base, conv, R, turns, out, out_modes, adv, modes, sems):
    circ, na, nt = R.shape[0], base.shape[1], base.shape[2]
    band = modes.shape[-1]
    lane = lax.broadcasted_iota(jnp.int32, (8, 128), 1)
    edge = lax.broadcasted_iota(jnp.int32, (8, 128), 0)

    fastest = R[0, SENT - 1 : SENT]
    for i in range(1, circ):
        fastest = jnp.maximum(fastest, R[i, SENT - 1 : SENT])
    step = 0.8 / (3.0 * jnp.broadcast_to(fastest, (nt, 128)))
    copies = []
    for f in range(FIELDS):
        for a in range(na):
            adv[f, a] = base[f, a] - step * conv[f, a]
        copies.append(pltpu.make_async_copy(adv.at[f], out.at[0, f], sems.at[f]))
        copies[-1].start()

    sums, tail = R[0, 0:8], R[0, 8 : SENT - 1]
    for i in range(1, circ):
        sums, tail = sums + R[i, 0:8], tail + R[i, 8 : SENT - 1]
    tail = jnp.concatenate([tail, jnp.zeros((17 - SENT, 128), F32)], axis=0)
    moved = pltpu.roll(sums, 128 - band * FIELDS, 1)
    for i in range(4):
        piece = pltpu.roll(tail, (band * 3 - 32 * i) % 128, 1)
        piece = pltpu.roll(piece, 2 * i, 0) if i else piece
        moved = jnp.where((edge // 2 == i) & (lane >= band * 3), piece, moved)
    own = sums - step[:8] * moved
    other = jnp.where(lax.rem(edge, 2) == 1, pltpu.roll(own, 1, 0), pltpu.roll(own, 7, 0))
    value = own * turns[0] + other * turns[1]
    for f in range(FIELDS):
        here = pltpu.roll(value, 128 - band * f, 1) if f else value
        for i in range(MODES_HERE):
            for part in range(2):
                row = 2 * i + part
                modes[0, i, f, part : part + 1] = here[row : row + 1, :band]
    copies.append(pltpu.make_async_copy(modes, out_modes, sems.at[FIELDS]))
    copies[-1].start()
    for copy in copies:
        copy.wait()


def on_device(circ, ax, state, rotor_step):
    na, nt = state.shape[2], state.shape[3]
    table = jnp.asarray(tables(circ, nt))
    hbm = pl.BlockSpec(memory_space=pltpu.HBM)
    vmem = pl.BlockSpec(memory_space=pltpu.VMEM)
    dma = pltpu.SemaphoreType.DMA
    block = (FIELDS, na, nt, 128)
    results = pl.pallas_call(
        functools.partial(comm_kernel, circ, 4 if circ % 4 == 0 else 1, ax),
        out_shape=[
            pltpu.VMEM(block, F32),
            pltpu.VMEM(block, F32),
            pltpu.VMEM((circ, 16, 128), F32),
            pltpu.VMEM((2, 8, 128), F32),
        ],
        in_specs=[hbm, hbm, hbm],
        out_specs=[vmem] * 4,
        scratch_shapes=[
            pltpu.VMEM((FIELDS, na + 2, nt, 128), F32),
            pltpu.VMEM((4, na + 2, nt, 128), F32),
            pltpu.VMEM((2, FIELDS, nt, 128), F32),
            pltpu.VMEM((2, FIELDS, na, 128), F32),
            pltpu.VMEM((2, FIELDS, na, 128), F32),
            pltpu.VMEM((circ * 8, DEPTH), F32),
            pltpu.VMEM((4, circ * 8, DEPTH), jnp.bfloat16),
            pltpu.VMEM((ax, BAND_ROWS, 128), F32),
            pltpu.VMEM((2, BAND_ROWS, 128), F32),
            pltpu.VMEM((2, circ, 16, 128), F32),
            pltpu.VMEM((1, 128), F32),
            pltpu.VMEM((2 * ax, 1, 128), F32),
            pltpu.SMEM((1, 1), jnp.int32),
            dma, dma, dma, dma((2,)), dma((2,)), dma((2,)), dma((2,)),
            dma, dma((2,)), dma, dma, dma((2,)), dma,
        ],
        compiler_params=pltpu.CompilerParams(
            collective_id=0, has_side_effects=True, vmem_limit_bytes=56 * 2**20
        ),
        name="exchange",
    )(state, rotor_step.reshape(1, 1), table)
    return pl.pallas_call(
        finish_kernel,
        out_shape=[
            jax.ShapeDtypeStruct(state.shape, F32),
            jax.ShapeDtypeStruct((1, MODES_HERE, FIELDS, 2, 128 // ax), F32),
        ],
        in_specs=[vmem] * 4,
        out_specs=[hbm, hbm],
        scratch_shapes=[
            pltpu.VMEM(block, F32),
            pltpu.VMEM((1, MODES_HERE, FIELDS, 2, 128 // ax), F32),
            dma((FIELDS + 1,)),
        ],
        compiler_params=pltpu.CompilerParams(vmem_limit_bytes=16 * 2**20),
        name="finish",
    )(*(pltpu.with_memory_space_constraint(v, pltpu.VMEM) for v in results))


def solution(mesh):
    return jax.shard_map(
        functools.partial(on_device, mesh.shape["circ"], mesh.shape["ax"]),
        mesh=mesh,
        in_specs=(P("row", None, "ax", "circ", None), P()),
        out_specs=(P("row", None, "ax", "circ", None), P("row", "circ", None, None, "ax")),
        check_vma=False,
    )
```
